32 devices in a mesh: groups: 2 (over y), tensor: 4 (over z), dp: 2 (over x), pair: 2 (over core).
Axes of the slice: x: 2, y: 2, z: 4, core: 2. Of those that a mesh axis runs over, the one named last changes fastest.
Arguments:
- tokens: bfloat16 [1024, 8192], P(('groups', 'dp', 'tensor')), parts along dimension 0, may hold values from -200 to 200
- time_order: int32 [1024], P(('groups', 'dp')), parts along dimension 0, may hold values from 0 to 255, as said below
- modality: int32 [1024], P(('groups', 'dp')), parts along dimension 0, may hold values 0 or 1
- norm_gain: float32 [2, 8192], replicated, may hold values from 0.5 to 2
- gate_weight: bfloat16 [8192, 16384], P('dp', ('tensor', 'pair')), may hold values from -0.0625 to 0.0625
- up_weight: bfloat16 [8192, 16384], P('dp', ('tensor', 'pair')), may hold values from -0.0625 to 0.0625
- down_weight: bfloat16 [16384, 8192], P(('tensor', 'pair'), 'dp'), may hold values from -0.046875 to 0.046875
Outputs:
- branch_out: bfloat16 [1024, 8192], P(('groups', 'dp', 'tensor', 'pair')), parts along dimension 0
The draws below stay inside these ranges and needn't reach their ends.
There are 2 independent parts, one for each index of `groups`. The reference program is written for one: setup_inputs(seed, part) draws one part's arguments, and reference() takes and returns one part's arrays. A program takes and returns all parts, laid end to end along the dimension named above; an argument that names none is the same for every part. Nothing has to cross between parts.
Inputs may be any that keep to these rules, and one draw needn't show every extreme that they name: `time_order`: within each aligned block of 256 rows, a permutation of 0 to 255.
All inputs are finite; a program needn't handle non-finite values. No bound on the sum of `modality` on one device may be relied on, other than what follows from the above.
Results may differ from the reference program's by a relative error of at most 0.014.
Values may be sent and summed in bfloat16 or wider, within the bound.
A program may use at most 320 MiB of HBM per device.

```python
import math
import jax
import jax.numpy as jnp
from jax import lax

D = 8192
FF_WIN = 16384
ROWS = 256
TOKENS = 512
FF_DEV = 2048
N_TENSOR = 4
N_PAIR = 2


def draw_tokens(key, part):
    key = jax.random.fold_in(key, 7)
    first_key, second_key, third_key = jax.random.split(key, 3)
    row_scale = jnp.exp(jax.random.uniform(first_key, (TOKENS, 1), jnp.float32, 0.0, math.log(10.0)))
    column_scale = jnp.exp(jax.random.uniform(second_key, (1, D), jnp.float32, math.log(0.5), math.log(5.0)))
    sample = jax.random.normal(third_key, (TOKENS, D), jnp.float32)
    sample = jnp.clip(sample, -4.0, 4.0)
    return (sample * row_scale * column_scale).astype(jnp.bfloat16)


def draw_time_order(key, part):
    key = jax.random.fold_in(key, 11)
    block_keys = jax.random.split(key, TOKENS // ROWS)
    orders = jax.vmap(lambda single: jax.random.permutation(single, ROWS))(block_keys)
    return orders.reshape(-1).astype(jnp.int32)


def set_ends(entries, key, low, largest):
    index_at = [jax.random.randint(jax.random.fold_in(key, axis), (), 0, length) for axis, length in enumerate(entries.shape)]
    widest = entries.shape.index(max(entries.shape))
    next_to = index_at[:widest] + [(index_at[widest] + 1) % entries.shape[widest]] + index_at[widest + 1:]
    return entries.at[tuple(index_at)].set(low).at[tuple(next_to)].set(largest)


def block_levels(key, shape, shards, smallest, high):
    loudness = 1.0
    for dim, shards_of in shards:
        draws = jax.random.uniform(jax.random.fold_in(jax.random.fold_in(key, 6), dim), (shards_of,), jnp.float32, smallest / len(shards), high / len(shards))
        loudness = loudness * jnp.repeat(jnp.exp(draws), shape[dim] // shards_of).reshape((-1,) + (1,) * (len(shape) - 1 - dim))
    return loudness


def centred(rng, shape, width, limit, shards=(), kind=jnp.bfloat16):
    gain = block_levels(rng, shape, shards, -0.22, 0.18) if shards else 1.0
    drawn = jax.random.normal(rng, shape, jnp.float32) * width * gain
    return jnp.minimum(jnp.maximum(drawn, -limit), limit).astype(kind)


def setup_inputs(seed: int = 0, part: int = 0) -> dict:
    key_of = jax.random.split(jax.random.key(seed), 8)
    part_keys = jax.random.split(jax.random.fold_in(key_of[7], part), 8)
    tokens = draw_tokens(jax.random.fold_in(jax.random.fold_in(key_of[7], part), 71), part)
    time_order = draw_time_order(jax.random.fold_in(jax.random.fold_in(key_of[7], part), 71), part)
    modality = set_ends((jax.random.randint(part_keys[2], (TOKENS,), 0, 3) < 1).astype(jnp.int32), jax.random.fold_in(part_keys[2], 1), 0, 1)
    norm_gain = jnp.clip(jnp.exp(jax.random.uniform(key_of[3], (2, D), jnp.float32, math.log(0.5), math.log(2.0))), 0.5, 2.0)
    gate_weight = centred(key_of[4], (D, FF_WIN), D ** -0.5, 0.0625, ((0, 2), (1, 8)))
    up_weight = centred(key_of[5], (D, FF_WIN), D ** -0.5, 0.0625, ((0, 2), (1, 8)))
    down_weight = centred(key_of[6], (FF_WIN, D), FF_WIN ** -0.5, 0.046875, ((0, 8), (1, 2)))
    return {"tokens": tokens, "time_order": time_order, "modality": modality, "norm_gain": norm_gain, "gate_weight": gate_weight, "up_weight": up_weight, "down_weight": down_weight}


EPSILON = 1e-05

def normalize(block_rows, row_kinds, norm_gain):
    values = block_rows.astype(jnp.float32)
    inverse_rms = lax.rsqrt(lax.optimization_barrier(jnp.mean(values * values, axis=1, keepdims=True)) + EPSILON)
    chosen = jnp.where(row_kinds[:, None] == 1, norm_gain[1][None, :], norm_gain[0][None, :])
    return (values * inverse_rms * chosen).astype(jnp.bfloat16)

def reference(tokens, time_order, modality, norm_gain, gate_weight, up_weight, down_weight):
    offsets = jnp.arange(TOKENS, dtype=jnp.int32) // ROWS * ROWS
    source = (offsets + time_order).astype(jnp.int32)
    sorted_rows = jnp.take(tokens, source, axis=0)
    row_kinds = jnp.take(modality, source, axis=0)
    normed = normalize(sorted_rows, row_kinds, norm_gain)
    gate_proj = jnp.dot(normed, gate_weight, preferred_element_type=jnp.float32)
    up_proj = jnp.dot(normed, up_weight, preferred_element_type=jnp.float32)
    hidden = (jax.nn.silu(gate_proj) * up_proj).astype(jnp.bfloat16)

    def add_block(totals, block_index):
        column_first = (block_index * FF_DEV).astype(jnp.int32)
        hidden_part = lax.dynamic_slice_in_dim(hidden, column_first, FF_DEV, 1)
        down_part = lax.dynamic_slice_in_dim(down_weight, column_first, FF_DEV, 0)
        partial_value = jnp.dot(hidden_part, down_part, preferred_element_type=jnp.float32).astype(jnp.bfloat16)
        partial_value = lax.optimization_barrier(partial_value)
        return (totals + partial_value.astype(jnp.float32), None)
    totals, _ = lax.scan(add_block, jnp.zeros((TOKENS, D), jnp.float32), jnp.arange(N_TENSOR * N_PAIR, dtype=jnp.int32))
    return totals.astype(jnp.bfloat16)
```

```python
import jax
import jax.numpy as jnp
from jax import lax
from jax.sharding import PartitionSpec as P

EPSILON = 1e-05


def normalize(block_rows, row_kinds, norm_gain):
    values = block_rows.astype(jnp.float32)
    inverse_rms = lax.rsqrt(jnp.mean(values * values, axis=1, keepdims=True) + EPSILON)
    chosen = jnp.where(row_kinds[:, None] == 1, norm_gain[1][None, :], norm_gain[0][None, :])
    return (values * inverse_rms * chosen).astype(jnp.bfloat16)


def exchange(pieces, n_dp):
    me = lax.axis_index("dp")
    got = jnp.zeros_like(pieces)
    got = lax.dynamic_update_index_in_dim(got, lax.dynamic_index_in_dim(pieces, me, 0, False), me, 0)
    for shift in range(1, n_dp):
        to = lax.rem(me + shift, n_dp)
        arrived = lax.ppermute(
            lax.dynamic_index_in_dim(pieces, to, 0, False),
            "dp",
            [(i, (i + shift) % n_dp) for i in range(n_dp)],
        )
        got = lax.dynamic_update_index_in_dim(got, arrived, lax.rem(me - shift + n_dp, n_dp), 0)
    return got


def spread(block, n_dp):
    me = lax.axis_index("dp")
    got = jnp.zeros((n_dp,) + block.shape, block.dtype)
    got = lax.dynamic_update_index_in_dim(got, block, me, 0)
    for shift in range(1, n_dp):
        arrived = lax.ppermute(block, "dp", [(i, (i + shift) % n_dp) for i in range(n_dp)])
        got = lax.dynamic_update_index_in_dim(got, arrived, lax.rem(me - shift + n_dp, n_dp), 0)
    return got


def plain(mesh, tokens, time_order, modality, norm_gain, gate_weight, up_weight, down_weight):
    n_dp, n_tensor, n_pair = mesh.shape["dp"], mesh.shape["tensor"], mesh.shape["pair"]
    held, width = tokens.shape
    rows = time_order.shape[0]
    depth, hidden_units = gate_weight.shape
    first = lax.axis_index("tensor") * held
    normed = normalize(tokens, lax.dynamic_slice_in_dim(modality, first, held, 0), norm_gain)
    by_part = normed.reshape(held, n_dp, depth).transpose(1, 0, 2)
    blocks = exchange(by_part, n_dp)
    every = lax.all_gather(blocks, "tensor", axis=1, tiled=True).reshape(n_dp * rows, depth)
    gate_part = jnp.dot(every, gate_weight, preferred_element_type=jnp.float32)
    up_part = jnp.dot(every, up_weight, preferred_element_type=jnp.float32)
    both = jnp.stack([gate_part, up_part]).reshape(2, n_dp, rows, hidden_units).transpose(1, 0, 2, 3)
    got = exchange(both.astype(jnp.bfloat16), n_dp).astype(jnp.float32)
    own = lax.axis_index("dp")
    mine = lax.dynamic_index_in_dim(both, own, 0, False)
    at = jnp.arange(n_dp)[:, None, None, None]
    summed = mine + jnp.sum(jnp.where(at == own, 0.0, got), axis=0)
    hidden = (jax.nn.silu(summed[0]) * summed[1]).astype(jnp.bfloat16)
    chosen = (time_order[:, None] == jnp.arange(rows)[None, :]).astype(jnp.bfloat16)
    hidden = jnp.dot(chosen, hidden, preferred_element_type=jnp.float32).astype(jnp.bfloat16)
    hidden = spread(hidden, n_dp).reshape(n_dp * rows, hidden_units)
    partial = jnp.dot(hidden, down_weight, preferred_element_type=jnp.float32).astype(jnp.bfloat16)
    partial = partial.reshape(n_dp, rows, -1)
    partial = lax.psum_scatter(partial, ("tensor", "pair"), scatter_dimension=1, tiled=True)
    return exchange(partial, n_dp).transpose(1, 0, 2).reshape(rows // (n_tensor * n_pair), width)


def solution(mesh):
    placed = (
        P(("groups", "dp", "tensor"), None),
        P(("groups", "dp")),
        P(("groups", "dp")),
        P(),
        P("dp", ("tensor", "pair")),
        P("dp", ("tensor", "pair")),
        P(("tensor", "pair"), "dp"),
    )

    def per_device(*arrays):
        return plain(mesh, *arrays)

    return jax.shard_map(
        per_device,
        mesh=mesh,
        in_specs=placed,
        out_specs=P(("groups", "dp", "tensor", "pair"), None),
        check_vma=False,
    )
```

```python
import jax
import jax.numpy as jnp
from jax import lax
from jax.experimental import pallas as pl
from jax.experimental.pallas import tpu as pltpu
from jax.sharding import PartitionSpec as P

EPSILON = 1e-05
BF, F32 = jnp.bfloat16, jnp.float32
MESH = pl.DeviceIdType.MESH


def normalize(block_rows, row_kinds, norm_gain):
    values = block_rows.astype(jnp.float32)
    inverse_rms = lax.rsqrt(jnp.mean(values * values, axis=1, keepdims=True) + EPSILON)
    chosen = jnp.where(row_kinds[:, None] == 1, norm_gain[1][None, :], norm_gain[0][None, :])
    return (values * inverse_rms * chosen).astype(jnp.bfloat16)


def exchange(pieces, n_dp):
    me = lax.axis_index("dp")
    got = jnp.zeros_like(pieces)
    got = lax.dynamic_update_index_in_dim(got, lax.dynamic_index_in_dim(pieces, me, 0, False), me, 0)
    for shift in range(1, n_dp):
        to = lax.rem(me + shift, n_dp)
        arrived = lax.ppermute(
            lax.dynamic_index_in_dim(pieces, to, 0, False),
            "dp",
            [(i, (i + shift) % n_dp) for i in range(n_dp)],
        )
        got = lax.dynamic_update_index_in_dim(got, arrived, lax.rem(me - shift + n_dp, n_dp), 0)
    return got


def spread(block, n_dp):
    me = lax.axis_index("dp")
    got = jnp.zeros((n_dp,) + block.shape, block.dtype)
    got = lax.dynamic_update_index_in_dim(got, block, me, 0)
    for shift in range(1, n_dp):
        arrived = lax.ppermute(block, "dp", [(i, (i + shift) % n_dp) for i in range(n_dp)])
        got = lax.dynamic_update_index_in_dim(got, arrived, lax.rem(me - shift + n_dp, n_dp), 0)
    return got


def plain(mesh, tokens, time_order, modality, norm_gain, gate_weight, up_weight, down_weight):
    n_dp, n_tensor, n_pair = mesh.shape["dp"], mesh.shape["tensor"], mesh.shape["pair"]
    held, width = tokens.shape
    rows = time_order.shape[0]
    depth, hidden_units = gate_weight.shape
    first = lax.axis_index("tensor") * held
    normed = normalize(tokens, lax.dynamic_slice_in_dim(modality, first, held, 0), norm_gain)
    by_part = normed.reshape(held, n_dp, depth).transpose(1, 0, 2)
    blocks = exchange(by_part, n_dp)
    every = lax.all_gather(blocks, "tensor", axis=1, tiled=True).reshape(n_dp * rows, depth)
    gate_part = jnp.dot(every, gate_weight, preferred_element_type=jnp.float32)
    up_part = jnp.dot(every, up_weight, preferred_element_type=jnp.float32)
    both = jnp.stack([gate_part, up_part]).reshape(2, n_dp, rows, hidden_units).transpose(1, 0, 2, 3)
    got = exchange(both.astype(jnp.bfloat16), n_dp).astype(jnp.float32)
    own = lax.axis_index("dp")
    mine = lax.dynamic_index_in_dim(both, own, 0, False)
    at = jnp.arange(n_dp)[:, None, None, None]
    summed = mine + jnp.sum(jnp.where(at == own, 0.0, got), axis=0)
    hidden = (jax.nn.silu(summed[0]) * summed[1]).astype(jnp.bfloat16)
    chosen = (time_order[:, None] == jnp.arange(rows)[None, :]).astype(jnp.bfloat16)
    hidden = jnp.dot(chosen, hidden, preferred_element_type=jnp.float32).astype(jnp.bfloat16)
    hidden = spread(hidden, n_dp).reshape(n_dp * rows, hidden_units)
    partial = jnp.dot(hidden, down_weight, preferred_element_type=jnp.float32).astype(jnp.bfloat16)
    partial = partial.reshape(n_dp, rows, -1)
    partial = lax.psum_scatter(partial, ("tensor", "pair"), scatter_dimension=1, tiled=True)
    return exchange(partial, n_dp).transpose(1, 0, 2).reshape(rows // (n_tensor * n_pair), width)


def fused(mesh, tokens, time_order, modality, norm_gain, gate_weight, up_weight, down_weight):
    n_z = mesh.shape["tensor"]
    held, width = tokens.shape
    rows = time_order.shape[0]
    depth, units = gate_weight.shape
    out_w = down_weight.shape[1]
    quarter = depth // 2
    wide = 256
    n_half = units // 2 // wide
    span = 512
    n_out = out_w // span
    half_rows = rows // 2
    share = half_rows // n_z

    def kernel(tok, kinds, order, gain, gw, uw, dw, out,
               xs, xg, order2, wgb, wdb, ps, pr, own, hid, sh, qs, qr, keep, zs, zr, acc, fs, fr,
               wsem, dsem, xs_s, xs_r, o_s, o_r, ag_s, ag_rz, ag_rp, p_s, p_r, h_s, h_r,
               q_s, q_r, z_s, z_r, f_s, f_r):
        x, z, c = lax.axis_index("dp"), lax.axis_index("tensor"), lax.axis_index("pair")
        ox, oc = 1 - x, 1 - c

        def remote(src, dst, send, recv, **to):
            return pltpu.make_async_remote_copy(
                src_ref=src, dst_ref=dst, send_sem=send, recv_sem=recv, device_id=to, device_id_type=MESH)

        def gu_copies(j, slot):
            col = pl.multiple_of(lax.rem(ox * n_half + j, 2 * n_half) * wide, wide)
            return (pltpu.make_async_copy(gw.at[:, pl.ds(col, wide)], wgb.at[slot, 0], wsem.at[slot, 0]),
                    pltpu.make_async_copy(uw.at[:, pl.ds(col, wide)], wgb.at[slot, 1], wsem.at[slot, 1]))

        def gu_start(j, slot):
            for copy in gu_copies(j, slot):
                copy.start()

        def down_copy(n, slot):
            col = pl.multiple_of(n * span, span)
            return pltpu.make_async_copy(dw.at[:, pl.ds(col, span)], wdb.at[slot], dsem.at[slot])

        gu_start(0, 0)
        down_copy(0, 0).start()

        barrier = pltpu.get_barrier_semaphore()
        pl.semaphore_signal(barrier, inc=1, device_id={"dp": ox}, device_id_type=MESH)
        pl.semaphore_signal(barrier, inc=1, device_id={"pair": oc}, device_id_type=MESH)
        for o in range(1, n_z):
            pl.semaphore_signal(barrier, inc=1, device_id={"tensor": lax.rem(z + o, n_z)}, device_id_type=MESH)

        def norm_step(i, _):
            at = pl.ds(pl.multiple_of(i * 16, 16), 16)
            values = tok[at, :].astype(F32)
            inverse = lax.rsqrt(jnp.mean(values * values, axis=1, keepdims=True) + EPSILON)
            kind = kinds[at, 0:1]

            def piece(first):
                cols = pl.ds(pl.multiple_of(first, quarter), quarter)
                chosen = jnp.where(kind == 1, gain[1:2, cols], gain[0:1, cols])
                return (tok[at, cols].astype(F32) * inverse * chosen).astype(BF)

            xs[at, :] = piece(ox * depth + c * quarter)
            place = pl.ds(pl.multiple_of(z * held + i * 16, 16), 16)
            for q in range(2):
                xg[x, q, place, :] = piece(x * depth + q * quarter)
            return 0

        lax.fori_loop(0, held // 16, norm_step, 0)
        pl.semaphore_wait(barrier, n_z + 1)

        def zrows(o):
            return pl.ds(pl.multiple_of(o * held, held), held)

        x_copy = remote(xs, xg.at[x, c, zrows(z)], xs_s, xs_r, dp=ox)
        x_copy.start()
        o_copy = remote(order, order2, o_s, o_r, dp=ox)
        o_copy.start()

        def ag(b, o, way):
            piece = xg.at[b, c, zrows(o)]
            if way == 2:
                return remote(piece, piece, ag_s.at[b, o, 2], ag_rp.at[b, o], pair=oc)
            to = lax.rem(z + (1 if way == 0 else n_z - 1), n_z)
            return remote(piece, piece, ag_s.at[b, o, way], ag_rz.at[b, o], tensor=to)

        def ag_each(b, d, act):
            if d == 0:
                pl.when(z < n_z - 1)(lambda: act(ag(b, z, 0)))
                pl.when(z > 0)(lambda: act(ag(b, z, 1)))
                pl.when(x != b)(lambda: act(ag(b, z, 2)))
                return
            left, right = lax.rem(z - d + n_z, n_z), lax.rem(z + d, n_z)
            pl.when((z >= d) & (z < n_z - 1))(lambda: act(ag(b, left, 0)))
            pl.when(z >= d)(lambda: act(ag(b, left, 2)))
            pl.when((z + d < n_z) & (z > 0))(lambda: act(ag(b, right, 1)))
            pl.when(z + d < n_z)(lambda: act(ag(b, right, 2)))

        def begin(copy):
            copy.start()

        def sent(copy):
            copy.wait_send()

        def own_sends(b):
            @pl.when(x != b)
            def _():
                remote(xs, xg.at[b, c, zrows(z)], xs_s, xs_r, dp=ox).wait_recv()
            ag_each(b, 0, begin)

        def hops(b):
            for d in range(1, n_z):
                left, right = lax.rem(z - d + n_z, n_z), lax.rem(z + d, n_z)
                pl.when(z >= d)(lambda: ag(b, left, 0).wait_recv())
                pl.when(z + d < n_z)(lambda: ag(b, right, 1).wait_recv())
                ag_each(b, d, begin)

        def sibling(b, o):
            piece = xg.at[b, oc, zrows(o)]
            remote(piece, piece, ag_s.at[b, o, 2], ag_rp.at[b, o], pair=oc).wait_recv()

        def siblings(b):
            pl.when(x != b)(lambda: sibling(b, z))
            for d in range(1, n_z):
                sibling(b, lax.rem(z + d, n_z))

        def p_copy(b, j):
            return remote(ps.at[b, j], pr.at[b, j], p_s.at[b, j], p_r.at[b, j], dp=ox)

        def gate_up(b):
            def step(j, _):
                slot = lax.rem(j, 2)
                if b == 0:
                    gu_start(lax.rem(j + 1, 2 * n_half), 1 - slot)
                else:
                    pl.when(j + 1 < 2 * n_half)(lambda: gu_start(j + 1, 1 - slot))
                for copy in gu_copies(j, slot):
                    copy.wait()
                got = []
                for m in range(2):
                    got.append(jnp.dot(xg[b, 0], wgb[slot, m, :quarter, :], preferred_element_type=F32)
                               + jnp.dot(xg[b, 1], wgb[slot, m, quarter:, :], preferred_element_type=F32))

                @pl.when(j < n_half)
                def _():
                    ps[b, j, 0] = got[0].astype(BF)
                    ps[b, j, 1] = got[1].astype(BF)
                    p_copy(b, j).start()

                @pl.when(j >= n_half)
                def _():
                    own[b, lax.rem(j, n_half), 0] = got[0]
                    own[b, lax.rem(j, n_half), 1] = got[1]
                return 0
            lax.fori_loop(0, 2 * n_half, step, 0)

        def h_copy(b, j, half):
            piece = hid.at[b, half * n_half + j]
            return remote(piece, piece, h_s.at[b, j], h_r.at[b, j], dp=ox)

        def hidden(b):
            def step(j, _):
                p_copy(b, j).wait_recv()
                gate = own[b, j, 0] + pr[b, j, 0].astype(F32)
                up = own[b, j, 1] + pr[b, j, 1].astype(F32)
                hid[b, x * n_half + j] = (gate / (1.0 + jnp.exp(-gate)) * up).astype(BF)
                h_copy(b, j, x).start()
                return 0
            lax.fori_loop(0, n_half, step, 0)

        def sort(b):
            at = jnp.where(x == b, order[...], order2[...])[0:1, :]
            match = (lax.broadcasted_iota(jnp.int32, (rows, rows), 0) == at).astype(F32)
            chosen = jnp.transpose(match).astype(BF)

            def step(j, _):
                h_copy(b, j, ox).wait_recv()
                return 0
            lax.fori_loop(0, n_half, step, 0)
            for k in range(2 * n_half):
                sh[:, k * wide:(k + 1) * wide] = jnp.dot(
                    chosen, hid[b, k], preferred_element_type=F32).astype(BF)

        def q_copy(b, n):
            return remote(qs.at[b, n], qr.at[b, n], q_s.at[b, n], q_r.at[b, n], pair=oc)

        def z_copy(b, n, o):
            to = lax.rem(z + o, n_z)
            return remote(zs.at[b, n, pl.ds(pl.multiple_of(to * share, share), share)], zr.at[b, n, z],
                          z_s.at[b, n, o], z_r.at[b, n, z], tensor=to)

        def z_arrival(b, n, o):
            src = lax.rem(z + o, n_z)
            return remote(zs.at[b, n, pl.ds(0, share)], zr.at[b, n, src],
                          z_s.at[b, n, o], z_r.at[b, n, src], tensor=src)

        def reduce(b, n):
            slot = lax.rem(n, 2)
            q_copy(b, n).wait_recv()
            total = keep[slot] + qr[b, n].astype(F32)
            zs[b, n] = total.astype(BF)
            for o in range(1, n_z):
                z_copy(b, n, o).start()
            keep[slot] = total
            acc[b, n] = keep[slot, pl.ds(pl.multiple_of(z * share, share), share), :]

        def down(b):
            def step(n, _):
                slot = lax.rem(n, 2)
                if b == 0:
                    down_copy(lax.rem(n + 1, n_out), 1 - slot).start()
                else:
                    pl.when(n + 1 < n_out)(lambda: down_copy(n + 1, 1 - slot).start())
                down_copy(n, slot).wait()
                part = jnp.dot(sh[...], wdb[slot], preferred_element_type=F32)
                qs[b, n] = part[half_rows:].astype(BF)
                q_copy(b, n).start()
                keep[slot] = part[:half_rows]
                pl.when(n >= 1)(lambda: reduce(b, n - 1))
                return 0
            lax.fori_loop(0, n_out, step, 0)
            reduce(b, n_out - 1)

        def f_copy(n):
            return remote(fs.at[n], fr.at[n], f_s.at[n], f_r.at[n], dp=ox)

        def finish(b):
            def step(n, _):
                total = acc[b, n]
                for o in range(1, n_z):
                    z_arrival(b, n, o).wait_recv()
                    total = total + zr[b, n, lax.rem(z + o, n_z)].astype(F32)

                @pl.when(x == b)
                def _():
                    out[:, pl.ds(pl.multiple_of(b * out_w + n * span, span), span)] = total.astype(BF)

                @pl.when(x != b)
                def _():
                    fs[n] = total.astype(BF)
                    f_copy(n).start()
                return 0
            lax.fori_loop(0, n_out, step, 0)

        own_sends(0)
        hops(0)
        own_sends(1)
        siblings(0)
        gate_up(0)
        hops(1)
        siblings(1)
        gate_up(1)
        hidden(0)
        o_copy.wait_recv()
        sort(0)
        down(0)
        hidden(1)
        sort(1)
        down(1)
        finish(0)
        finish(1)

        def last(n, _):
            f_copy(n).wait_recv()
            out[:, pl.ds(pl.multiple_of(ox * out_w + n * span, span), span)] = fr[n]
            return 0
        lax.fori_loop(0, n_out, last, 0)

        x_copy.wait_send()
        o_copy.wait_send()
        for b in range(2):
            for d in range(n_z):
                ag_each(b, d, sent)

            def sent_x(j, _):
                p_copy(b, j).wait_send()
                h_copy(b, j, x).wait_send()
                return 0
            lax.fori_loop(0, n_half, sent_x, 0)

            def sent_z(n, _):
                q_copy(b, n).wait_send()
                for o in range(1, n_z):
                    z_copy(b, n, o).wait_send()
                return 0
            lax.fori_loop(0, n_out, sent_z, 0)

        def sent_f(n, _):
            f_copy(n).wait_send()
            return 0
        lax.fori_loop(0, n_out, sent_f, 0)

    z, c = lax.axis_index("tensor"), lax.axis_index("pair")
    kinds = lax.dynamic_slice_in_dim(modality, z * held, held, 0)
    kinds = jnp.broadcast_to(kinds[:, None], (held, 128))
    order = time_order.reshape(n_z, 2, share).transpose(1, 0, 2)
    order = jnp.where(c == 0, order, order[::-1]).reshape(1, rows)
    order = jnp.broadcast_to(order, (8, rows))
    vmem, anywhere = pl.BlockSpec(memory_space=pltpu.VMEM), pl.BlockSpec(memory_space=pl.ANY)
    dma = pltpu.SemaphoreType.DMA
    scratch = [
        pltpu.VMEM((held, quarter), BF),
        pltpu.VMEM((2, 2, rows, quarter), BF),
        pltpu.VMEM((8, rows), jnp.int32),
        pltpu.VMEM((2, 2, depth, wide), BF),
        pltpu.VMEM((2, units, span), BF),
        pltpu.VMEM((2, n_half, 2, rows, wide), BF),
        pltpu.VMEM((2, n_half, 2, rows, wide), BF),
        pltpu.VMEM((2, n_half, 2, rows, wide), F32),
        pltpu.VMEM((2, 2 * n_half, rows, wide), BF),
        pltpu.VMEM((rows, units), BF),
        pltpu.VMEM((2, n_out, half_rows, span), BF),
        pltpu.VMEM((2, n_out, half_rows, span), BF),
        pltpu.VMEM((2, half_rows, span), F32),
        pltpu.VMEM((2, n_out, half_rows, span), BF),
        pltpu.VMEM((2, n_out, n_z, share, span), BF),
        pltpu.VMEM((2, n_out, share, span), F32),
        pltpu.VMEM((n_out, share, span), BF),
        pltpu.VMEM((n_out, share, span), BF),
        dma((2, 2)), dma((2,)), dma, dma, dma, dma,
        dma((2, n_z, 3)), dma((2, n_z)), dma((2, n_z)),
        dma((2, n_half)), dma((2, n_half)), dma((2, n_half)), dma((2, n_half)),
        dma((2, n_out)), dma((2, n_out)), dma((2, n_out, n_z)), dma((2, n_out, n_z)),
        dma((n_out,)), dma((n_out,)),
    ]
    return pl.pallas_call(
        kernel,
        out_shape=jax.ShapeDtypeStruct((rows // (n_z * 2), width), BF),
        in_specs=[vmem, vmem, vmem, vmem, anywhere, anywhere, anywhere],
        out_specs=vmem,
        scratch_shapes=scratch,
        compiler_params=pltpu.CompilerParams(
            collective_id=0, has_side_effects=True, vmem_limit_bytes=58 * 2**20),
        cost_estimate=pl.CostEstimate(
            flops=12 * rows * depth * units, bytes_accessed=12 * depth * units, transcendentals=0),
    )(tokens, kinds, order, norm_gain, gate_weight, up_weight, down_weight)


def solution(mesh):
    placed = (
        P(("groups", "dp", "tensor"), None),
        P(("groups", "dp")),
        P(("groups", "dp")),
        P(),
        P("dp", ("tensor", "pair")),
        P("dp", ("tensor", "pair")),
        P(("tensor", "pair"), "dp"),
    )

    def per_device(*arrays):
        share = arrays[1].shape[0] // (mesh.shape["tensor"] * mesh.shape["pair"])
        if mesh.shape["dp"] == 2 and mesh.shape["pair"] == 2 and share % 16 == 0:
            return fused(mesh, *arrays)
        return plain(mesh, *arrays)

    return jax.shard_map(
        per_device,
        mesh=mesh,
        in_specs=placed,
        out_specs=P(("groups", "dp", "tensor", "pair"), None),
        check_vma=False,
    )
```

```python
import jax
import jax.numpy as jnp
from jax import lax
from jax.experimental import pallas as pl
from jax.experimental.pallas import tpu as pltpu
from jax.sharding import PartitionSpec as P

EPSILON = 1e-05
BF, F32 = jnp.bfloat16, jnp.float32
MESH = pl.DeviceIdType.MESH


def normalize(block_rows, row_kinds, norm_gain):
    values = block_rows.astype(jnp.float32)
    inverse_rms = lax.rsqrt(jnp.mean(values * values, axis=1, keepdims=True) + EPSILON)
    chosen = jnp.where(row_kinds[:, None] == 1, norm_gain[1][None, :], norm_gain[0][None, :])
    return (values * inverse_rms * chosen).astype(jnp.bfloat16)


def exchange(pieces, n_dp):
    me = lax.axis_index("dp")
    got = jnp.zeros_like(pieces)
    got = lax.dynamic_update_index_in_dim(got, lax.dynamic_index_in_dim(pieces, me, 0, False), me, 0)
    for shift in range(1, n_dp):
        to = lax.rem(me + shift, n_dp)
        arrived = lax.ppermute(
            lax.dynamic_index_in_dim(pieces, to, 0, False),
            "dp",
            [(i, (i + shift) % n_dp) for i in range(n_dp)],
        )
        got = lax.dynamic_update_index_in_dim(got, arrived, lax.rem(me - shift + n_dp, n_dp), 0)
    return got


def spread(block, n_dp):
    me = lax.axis_index("dp")
    got = jnp.zeros((n_dp,) + block.shape, block.dtype)
    got = lax.dynamic_update_index_in_dim(got, block, me, 0)
    for shift in range(1, n_dp):
        arrived = lax.ppermute(block, "dp", [(i, (i + shift) % n_dp) for i in range(n_dp)])
        got = lax.dynamic_update_index_in_dim(got, arrived, lax.rem(me - shift + n_dp, n_dp), 0)
    return got


def plain(mesh, tokens, time_order, modality, norm_gain, gate_weight, up_weight, down_weight):
    n_dp, n_tensor, n_pair = mesh.shape["dp"], mesh.shape["tensor"], mesh.shape["pair"]
    held, width = tokens.shape
    rows = time_order.shape[0]
    depth, hidden_units = gate_weight.shape
    first = lax.axis_index("tensor") * held
    normed = normalize(tokens, lax.dynamic_slice_in_dim(modality, first, held, 0), norm_gain)
    by_part = normed.reshape(held, n_dp, depth).transpose(1, 0, 2)
    blocks = exchange(by_part, n_dp)
    every = lax.all_gather(blocks, "tensor", axis=1, tiled=True).reshape(n_dp * rows, depth)
    gate_part = jnp.dot(every, gate_weight, preferred_element_type=jnp.float32)
    up_part = jnp.dot(every, up_weight, preferred_element_type=jnp.float32)
    both = jnp.stack([gate_part, up_part]).reshape(2, n_dp, rows, hidden_units).transpose(1, 0, 2, 3)
    got = exchange(both.astype(jnp.bfloat16), n_dp).astype(jnp.float32)
    own = lax.axis_index("dp")
    mine = lax.dynamic_index_in_dim(both, own, 0, False)
    at = jnp.arange(n_dp)[:, None, None, None]
    summed = mine + jnp.sum(jnp.where(at == own, 0.0, got), axis=0)
    hidden = (jax.nn.silu(summed[0]) * summed[1]).astype(jnp.bfloat16)
    chosen = (time_order[:, None] == jnp.arange(rows)[None, :]).astype(jnp.bfloat16)
    hidden = jnp.dot(chosen, hidden, preferred_element_type=jnp.float32).astype(jnp.bfloat16)
    hidden = spread(hidden, n_dp).reshape(n_dp * rows, hidden_units)
    partial = jnp.dot(hidden, down_weight, preferred_element_type=jnp.float32).astype(jnp.bfloat16)
    partial = partial.reshape(n_dp, rows, -1)
    partial = lax.psum_scatter(partial, ("tensor", "pair"), scatter_dimension=1, tiled=True)
    return exchange(partial, n_dp).transpose(1, 0, 2).reshape(rows // (n_tensor * n_pair), width)


def fused(mesh, tokens, time_order, modality, norm_gain, gate_weight, up_weight, down_weight):
    n_z = mesh.shape["tensor"]
    held, width = tokens.shape
    rows = time_order.shape[0]
    depth, units = gate_weight.shape
    out_w = down_weight.shape[1]
    quarter = depth // 2
    wide = 256
    n_half = units // 2 // wide
    span = 512
    n_out = out_w // span
    half_rows = rows // 2
    near = n_z // 2
    kept = half_rows // 2
    share = kept // n_z

    def kernel(tok, kinds, order, gain, gw, uw, dw, out,
               xs, xg, xt, order2, wgb, wdb, ps, pr, own, hid, sh, qs, qr, keep, zs, zr, acc, fs, fr,
               wsem, dsem, xs_s, xs_r, o_s, o_r, ag_s, ag_rz, ag_rp, p_s, p_r, h_s, h_r,
               q_s, q_r, z_s, z_r, f_s, f_r):
        x, z, c = lax.axis_index("dp"), lax.axis_index("tensor"), lax.axis_index("pair")
        ox, oc = 1 - x, 1 - c

        def remote(src, dst, send, recv, **to):
            return pltpu.make_async_remote_copy(
                src_ref=src, dst_ref=dst, send_sem=send, recv_sem=recv, device_id=to, device_id_type=MESH)

        def gu_copies(j, slot):
            col = pl.multiple_of(lax.rem(ox * n_half + j, 2 * n_half) * wide, wide)
            return (pltpu.make_async_copy(gw.at[:, pl.ds(col, wide)], wgb.at[slot, 0], wsem.at[slot, 0]),
                    pltpu.make_async_copy(uw.at[:, pl.ds(col, wide)], wgb.at[slot, 1], wsem.at[slot, 1]))

        def gu_start(j, slot):
            for copy in gu_copies(j, slot):
                copy.start()

        def down_copy(n, slot):
            col = pl.multiple_of(n * span, span)
            return pltpu.make_async_copy(dw.at[:, pl.ds(col, span)], wdb.at[slot], dsem.at[slot])

        gu_start(0, 0)
        down_copy(0, 0).start()

        barrier = pltpu.get_barrier_semaphore()
        pl.semaphore_signal(barrier, inc=1, device_id={"dp": ox}, device_id_type=MESH)
        pl.semaphore_signal(barrier, inc=1, device_id={"pair": oc}, device_id_type=MESH)
        for o in range(1, n_z):
            pl.semaphore_signal(barrier, inc=1, device_id={"tensor": lax.rem(z + o, n_z)}, device_id_type=MESH)

        def norm_step(i, _):
            at = pl.ds(pl.multiple_of(i * 16, 16), 16)
            values = tok[at, :].astype(F32)
            inverse = lax.rsqrt(jnp.mean(values * values, axis=1, keepdims=True) + EPSILON)
            kind = kinds[at, 0:1]

            def piece(first):
                cols = pl.ds(pl.multiple_of(first, quarter), quarter)
                chosen = jnp.where(kind == 1, gain[1:2, cols], gain[0:1, cols])
                return (tok[at, cols].astype(F32) * inverse * chosen).astype(BF)

            xs[at, :] = piece(ox * depth + c * quarter)
            place = pl.ds(pl.multiple_of(z * held + i * 16, 16), 16)
            for q in range(2):
                xg[x, q, place, :] = piece(x * depth + q * quarter)
            return 0

        lax.fori_loop(0, held // 16, norm_step, 0)
        pl.semaphore_wait(barrier, n_z + 1)

        def zrows(o):
            return pl.ds(pl.multiple_of(o * held, held), held)

        x_copy = remote(xs, xg.at[x, c, zrows(z)], xs_s, xs_r, dp=ox)
        x_copy.start()
        o_copy = remote(order, order2, o_s, o_r, dp=ox)
        o_copy.start()

        def ag(b, o, way):
            piece = xg.at[b, c, zrows(o)]
            if way == 2:
                return remote(piece, piece, ag_s.at[b, o, 2], ag_rp.at[b, o], pair=oc)
            to = lax.rem(z + (1 if way == 0 else n_z - 1), n_z)
            return remote(piece, piece, ag_s.at[b, o, way], ag_rz.at[b, o], tensor=to)

        def ag_each(b, d, act):
            if d == 0:
                pl.when(z < n_z - 1)(lambda: act(ag(b, z, 0)))
                pl.when(z > 0)(lambda: act(ag(b, z, 1)))
                pl.when(x != b)(lambda: act(ag(b, z, 2)))
                return
            left, right = lax.rem(z - d + n_z, n_z), lax.rem(z + d, n_z)
            pl.when((z >= d) & (z < n_z - 1))(lambda: act(ag(b, left, 0)))
            pl.when(z >= d)(lambda: act(ag(b, left, 2)))
            pl.when((z + d < n_z) & (z > 0))(lambda: act(ag(b, right, 1)))
            pl.when(z + d < n_z)(lambda: act(ag(b, right, 2)))

        def begin(copy):
            copy.start()

        def sent(copy):
            copy.wait_send()

        def own_sends(b):
            @pl.when(x != b)
            def _():
                remote(xs, xg.at[b, c, zrows(z)], xs_s, xs_r, dp=ox).wait_recv()
            ag_each(b, 0, begin)

        def hop(b, d):
            left, right = lax.rem(z - d + n_z, n_z), lax.rem(z + d, n_z)
            pl.when(z >= d)(lambda: ag(b, left, 0).wait_recv())
            pl.when(z + d < n_z)(lambda: ag(b, right, 1).wait_recv())
            ag_each(b, d, begin)

        def sibling(b, o):
            piece = xg.at[b, oc, zrows(o)]
            remote(piece, piece, ag_s.at[b, o, 2], ag_rp.at[b, o], pair=oc).wait_recv()

        def siblings(b, half):
            for k in range(near):
                o = half * near + k
                pl.when((x != b) | (o != z))(lambda: sibling(b, o))

        def p_copy(u, j):
            return remote(ps.at[u, j], pr.at[u, j], p_s.at[u, j], p_r.at[u, j], dp=ox)

        def gate_up(u, rows_of, part, final=False):
            def step(j, _):
                slot = lax.rem(j, 2)
                if final:
                    pl.when(j + 1 < 2 * n_half)(lambda: gu_start(j + 1, 1 - slot))
                else:
                    gu_start(lax.rem(j + 1, 2 * n_half), 1 - slot)
                for copy in gu_copies(j, slot):
                    copy.wait()
                for m in range(2):
                    got = (jnp.dot(rows_of(0), wgb[slot, m, :quarter, :], preferred_element_type=F32)
                           + jnp.dot(rows_of(1), wgb[slot, m, quarter:, :], preferred_element_type=F32))
                    if part == 0:
                        ps[u, j, m] = got.astype(BF)
                    else:
                        own[u, j - n_half, m] = got
                if part == 0:
                    p_copy(u, j).start()
                return 0
            lax.fori_loop(part * n_half, (part + 1) * n_half, step, 0)

        def arrived(half):
            at = pl.ds(pl.multiple_of(half * half_rows, half_rows), half_rows)
            return lambda q: xg[0, q, at, :]

        def h_copy(u, j, half):
            piece = hid.at[u, half * n_half + j]
            return remote(piece, piece, h_s.at[u, j], h_r.at[u, j], dp=ox)

        def hidden(u):
            def step(j, _):
                p_copy(u, j).wait_recv()
                gate = own[u, j, 0] + pr[u, j, 0].astype(F32)
                up = own[u, j, 1] + pr[u, j, 1].astype(F32)
                hid[u, x * n_half + j] = (gate / (1.0 + jnp.exp(-gate)) * up).astype(BF)
                h_copy(u, j, x).start()
                return 0
            lax.fori_loop(0, n_half, step, 0)

        def hidden_arrival(u):
            def step(j, _):
                h_copy(u, j, ox).wait_recv()
                return 0
            lax.fori_loop(0, n_half, step, 0)

        def chooser(b):
            at = jnp.where(x == b, order[...], order2[...])[0:1, :]
            match = (lax.broadcasted_iota(jnp.int32, (rows, rows), 0) == at).astype(F32)
            return jnp.transpose(match).astype(BF)

        def sort_hidden():
            chosen = chooser(0)
            for k in range(2 * n_half):
                sh[:, k * wide:(k + 1) * wide] = (
                    jnp.dot(chosen[:, :half_rows], hid[0, k], preferred_element_type=F32)
                    + jnp.dot(chosen[:, half_rows:], hid[1, k], preferred_element_type=F32)).astype(BF)

        def sort_tokens():
            chosen = chooser(1)
            for q in range(2):
                for k in range(0, quarter, span):
                    moved = jnp.dot(chosen, xg[1, q, :, k:k + span], preferred_element_type=F32).astype(BF)
                    xt[0, q, :, k:k + span] = moved[:half_rows]
                    xt[1, q, :, k:k + span] = moved[half_rows:]

        def in_order(u):
            for k in range(2 * n_half):
                sh[:half_rows, k * wide:(k + 1) * wide] = hid[u, k]

        def q_copy(u, n):
            return remote(qs.at[u, n], qr.at[u, n], q_s.at[u, n], q_r.at[u, n], pair=oc)

        def z_copy(u, n, o):
            to = lax.rem(z + o, n_z)
            return remote(zs.at[u, n, pl.ds(pl.multiple_of(to * share, share), share)], zr.at[u, n, z],
                          z_s.at[u, n, o], z_r.at[u, n, z], tensor=to)

        def z_arrival(u, n, o):
            src = lax.rem(z + o, n_z)
            return remote(zs.at[u, n, pl.ds(0, share)], zr.at[u, n, src],
                          z_s.at[u, n, o], z_r.at[u, n, src], tensor=src)

        def reduce(units_of, n):
            slot = lax.rem(n, 2)
            for i, u in enumerate(units_of):
                q_copy(u, n).wait_recv()
                total = keep[slot, i] + qr[u, n].astype(F32)
                zs[u, n] = total.astype(BF)
                for o in range(1, n_z):
                    z_copy(u, n, o).start()
                keep[slot, i] = total
                acc[u, n] = keep[slot, i, pl.ds(pl.multiple_of(z * share, share), share), :]

        def down(units_of, final=False):
            many = len(units_of)

            def step(n, _):
                slot = lax.rem(n, 2)
                if final:
                    pl.when(n + 1 < n_out)(lambda: down_copy(n + 1, 1 - slot).start())
                else:
                    down_copy(lax.rem(n + 1, n_out), 1 - slot).start()
                down_copy(n, slot).wait()
                part = jnp.dot(sh[:many * half_rows, :], wdb[slot], preferred_element_type=F32)
                for i, u in enumerate(units_of):
                    qs[u, n] = part[i * half_rows + kept:(i + 1) * half_rows].astype(BF)
                    q_copy(u, n).start()
                    keep[slot, i] = part[i * half_rows:i * half_rows + kept]
                pl.when(n >= 1)(lambda: reduce(units_of, n - 1))
                return 0
            lax.fori_loop(0, n_out, step, 0)
            reduce(units_of, n_out - 1)

        def f_copy(h, n):
            return remote(fs.at[h, n], fr.at[h, n], f_s.at[h, n], f_r.at[h, n], dp=ox)

        def finish(u):
            b, h = u // 2, u % 2

            def step(n, _):
                total = acc[u, n]
                for o in range(1, n_z):
                    z_arrival(u, n, o).wait_recv()
                    total = total + zr[u, n, lax.rem(z + o, n_z)].astype(F32)

                @pl.when(x == b)
                def _():
                    out[h * share:(h + 1) * share,
                        pl.ds(pl.multiple_of(b * out_w + n * span, span), span)] = total.astype(BF)

                @pl.when(x != b)
                def _():
                    fs[h, n] = total.astype(BF)
                    f_copy(h, n).start()
                return 0
            lax.fori_loop(0, n_out, step, 0)

        side = z // near
        own_sends(0)
        for d in range(1, near):
            hop(0, d)
        siblings(0, side)
        gate_up(side, arrived(side), 0)
        hop(0, near)
        gate_up(side, arrived(side), 1)
        for d in range(near + 1, n_z):
            hop(0, d)
        own_sends(1)
        siblings(0, 1 - side)
        gate_up(1 - side, arrived(1 - side), 0)
        for d in range(1, near):
            hop(1, d)
        gate_up(1 - side, arrived(1 - side), 1)
        hop(1, near)
        hidden(side)
        for d in range(near + 1, n_z):
            hop(1, d)
        siblings(1, 0)
        siblings(1, 1)
        o_copy.wait_recv()
        sort_tokens()
        hidden(1 - side)
        gate_up(2, lambda q: xt[0, q], 0)
        gate_up(2, lambda q: xt[0, q], 1)
        hidden_arrival(0)
        hidden_arrival(1)
        sort_hidden()
        down((0, 1))
        gate_up(3, lambda q: xt[1, q], 0)
        gate_up(3, lambda q: xt[1, q], 1, True)
        hidden(2)
        hidden(3)
        finish(0)
        finish(1)
        hidden_arrival(2)
        in_order(2)
        down((2,))
        hidden_arrival(3)
        in_order(3)
        down((3,), True)
        finish(2)
        finish(3)

        for h in range(2):
            def last(n, _):
                f_copy(h, n).wait_recv()
                out[h * share:(h + 1) * share,
                    pl.ds(pl.multiple_of(ox * out_w + n * span, span), span)] = fr[h, n]
                return 0
            lax.fori_loop(0, n_out, last, 0)

        x_copy.wait_send()
        o_copy.wait_send()
        for b in range(2):
            for d in range(n_z):
                ag_each(b, d, sent)

        def sent_unit(u, _):
            def sent_x(j, _):
                p_copy(u, j).wait_send()
                h_copy(u, j, x).wait_send()
                return 0
            lax.fori_loop(0, n_half, sent_x, 0)

            def sent_z(n, _):
                q_copy(u, n).wait_send()
                for o in range(1, n_z):
                    z_copy(u, n, o).wait_send()
                return 0
            lax.fori_loop(0, n_out, sent_z, 0)
            return 0
        lax.fori_loop(0, 4, sent_unit, 0)

        def sent_f(n, _):
            f_copy(0, n).wait_send()
            f_copy(1, n).wait_send()
            return 0
        lax.fori_loop(0, n_out, sent_f, 0)

    z, c = lax.axis_index("tensor"), lax.axis_index("pair")
    kinds = lax.dynamic_slice_in_dim(modality, z * held, held, 0)
    kinds = jnp.broadcast_to(kinds[:, None], (held, 128))
    order = time_order.reshape(n_z, 2, 2, share).transpose(2, 1, 0, 3)
    order = jnp.where(c == 0, order, order[:, ::-1]).reshape(1, rows)
    order = jnp.broadcast_to(order, (8, rows))
    vmem, anywhere = pl.BlockSpec(memory_space=pltpu.VMEM), pl.BlockSpec(memory_space=pl.ANY)
    dma = pltpu.SemaphoreType.DMA
    scratch = [
        pltpu.VMEM((held, quarter), BF),
        pltpu.VMEM((2, 2, rows, quarter), BF),
        pltpu.VMEM((2, 2, half_rows, quarter), BF),
        pltpu.VMEM((8, rows), jnp.int32),
        pltpu.VMEM((2, 2, depth, wide), BF),
        pltpu.VMEM((2, units, span), BF),
        pltpu.VMEM((4, n_half, 2, half_rows, wide), BF),
        pltpu.VMEM((4, n_half, 2, half_rows, wide), BF),
        pltpu.VMEM((4, n_half, 2, half_rows, wide), F32),
        pltpu.VMEM((4, 2 * n_half, half_rows, wide), BF),
        pltpu.VMEM((rows, units), BF),
        pltpu.VMEM((4, n_out, kept, span), BF),
        pltpu.VMEM((4, n_out, kept, span), BF),
        pltpu.VMEM((2, 2, kept, span), F32),
        pltpu.VMEM((4, n_out, kept, span), BF),
        pltpu.VMEM((4, n_out, n_z, share, span), BF),
        pltpu.VMEM((4, n_out, share, span), F32),
        pltpu.VMEM((2, n_out, share, span), BF),
        pltpu.VMEM((2, n_out, share, span), BF),
        dma((2, 2)), dma((2,)), dma, dma, dma, dma,
        dma((2, n_z, 3)), dma((2, n_z)), dma((2, n_z)),
        dma((4, n_half)), dma((4, n_half)), dma((4, n_half)), dma((4, n_half)),
        dma((4, n_out)), dma((4, n_out)), dma((4, n_out, n_z)), dma((4, n_out, n_z)),
        dma((2, n_out)), dma((2, n_out)),
    ]
    return pl.pallas_call(
        kernel,
        out_shape=jax.ShapeDtypeStruct((rows // (n_z * 2), width), BF),
        in_specs=[vmem, vmem, vmem, vmem, anywhere, anywhere, anywhere],
        out_specs=vmem,
        scratch_shapes=scratch,
        compiler_params=pltpu.CompilerParams(
            collective_id=0, has_side_effects=True, vmem_limit_bytes=58 * 2**20),
        cost_estimate=pl.CostEstimate(
            flops=12 * rows * depth * units, bytes_accessed=12 * depth * units, transcendentals=0),
    )(tokens, kinds, order, norm_gain, gate_weight, up_weight, down_weight)


def solution(mesh):
    placed = (
        P(("groups", "dp", "tensor"), None),
        P(("groups", "dp")),
        P(("groups", "dp")),
        P(),
        P("dp", ("tensor", "pair")),
        P("dp", ("tensor", "pair")),
        P(("tensor", "pair"), "dp"),
    )

    def per_device(*arrays):
        share = arrays[1].shape[0] // (mesh.shape["tensor"] * mesh.shape["pair"])
        if mesh.shape["dp"] == 2 and mesh.shape["pair"] == 2 and share % 32 == 0:
            return fused(mesh, *arrays)
        return plain(mesh, *arrays)

    return jax.shard_map(
        per_device,
        mesh=mesh,
        in_specs=placed,
        out_specs=P(("groups", "dp", "tensor", "pair"), None),
        check_vma=False,
    )
```

```python
import jax
import jax.numpy as jnp
from jax import lax
from jax.experimental import pallas as pl
from jax.experimental.pallas import tpu as pltpu
from jax.sharding import PartitionSpec as P

EPSILON = 1e-05
BF, F32 = jnp.bfloat16, jnp.float32
MESH = pl.DeviceIdType.MESH


def normalize(block_rows, row_kinds, norm_gain):
    values = block_rows.astype(jnp.float32)
    inverse_rms = lax.rsqrt(jnp.mean(values * values, axis=1, keepdims=True) + EPSILON)
    chosen = jnp.where(row_kinds[:, None] == 1, norm_gain[1][None, :], norm_gain[0][None, :])
    return (values * inverse_rms * chosen).astype(jnp.bfloat16)


def exchange(pieces, n_dp):
    me = lax.axis_index("dp")
    got = jnp.zeros_like(pieces)
    got = lax.dynamic_update_index_in_dim(got, lax.dynamic_index_in_dim(pieces, me, 0, False), me, 0)
    for shift in range(1, n_dp):
        to = lax.rem(me + shift, n_dp)
        arrived = lax.ppermute(
            lax.dynamic_index_in_dim(pieces, to, 0, False),
            "dp",
            [(i, (i + shift) % n_dp) for i in range(n_dp)],
        )
        got = lax.dynamic_update_index_in_dim(got, arrived, lax.rem(me - shift + n_dp, n_dp), 0)
    return got


def spread(block, n_dp):
    me = lax.axis_index("dp")
    got = jnp.zeros((n_dp,) + block.shape, block.dtype)
    got = lax.dynamic_update_index_in_dim(got, block, me, 0)
    for shift in range(1, n_dp):
        arrived = lax.ppermute(block, "dp", [(i, (i + shift) % n_dp) for i in range(n_dp)])
        got = lax.dynamic_update_index_in_dim(got, arrived, lax.rem(me - shift + n_dp, n_dp), 0)
    return got


def plain(mesh, tokens, time_order, modality, norm_gain, gate_weight, up_weight, down_weight):
    n_dp, n_tensor, n_pair = mesh.shape["dp"], mesh.shape["tensor"], mesh.shape["pair"]
    held, width = tokens.shape
    rows = time_order.shape[0]
    depth, hidden_units = gate_weight.shape
    first = lax.axis_index("tensor") * held
    normed = normalize(tokens, lax.dynamic_slice_in_dim(modality, first, held, 0), norm_gain)
    by_part = normed.reshape(held, n_dp, depth).transpose(1, 0, 2)
    blocks = exchange(by_part, n_dp)
    every = lax.all_gather(blocks, "tensor", axis=1, tiled=True).reshape(n_dp * rows, depth)
    gate_part = jnp.dot(every, gate_weight, preferred_element_type=jnp.float32)
    up_part = jnp.dot(every, up_weight, preferred_element_type=jnp.float32)
    both = jnp.stack([gate_part, up_part]).reshape(2, n_dp, rows, hidden_units).transpose(1, 0, 2, 3)
    got = exchange(both.astype(jnp.bfloat16), n_dp).astype(jnp.float32)
    own = lax.axis_index("dp")
    mine = lax.dynamic_index_in_dim(both, own, 0, False)
    at = jnp.arange(n_dp)[:, None, None, None]
    summed = mine + jnp.sum(jnp.where(at == own, 0.0, got), axis=0)
    hidden = (jax.nn.silu(summed[0]) * summed[1]).astype(jnp.bfloat16)
    chosen = (time_order[:, None] == jnp.arange(rows)[None, :]).astype(jnp.bfloat16)
    hidden = jnp.dot(chosen, hidden, preferred_element_type=jnp.float32).astype(jnp.bfloat16)
    hidden = spread(hidden, n_dp).reshape(n_dp * rows, hidden_units)
    partial = jnp.dot(hidden, down_weight, preferred_element_type=jnp.float32).astype(jnp.bfloat16)
    partial = partial.reshape(n_dp, rows, -1)
    partial = lax.psum_scatter(partial, ("tensor", "pair"), scatter_dimension=1, tiled=True)
    return exchange(partial, n_dp).transpose(1, 0, 2).reshape(rows // (n_tensor * n_pair), width)


def fused(mesh, tokens, time_order, modality, norm_gain, gate_weight, up_weight, down_weight):
    n_z = mesh.shape["tensor"]
    held, width = tokens.shape
    rows = time_order.shape[0]
    depth, units = gate_weight.shape
    out_w = down_weight.shape[1]
    quarter = depth // 2
    wide = 256
    n_half = units // 2 // wide
    span = 512
    n_out = out_w // span
    half_rows = rows // 2
    near = n_z // 2
    kept = half_rows // 2
    share = kept // n_z

    def kernel(tok, kinds, order, gain, gw, uw, dw, out,
               xs, xg, xt, order2, wgb, wdb, ps, pr, own, hid, sh, qs, qr, keep, zs, zr, acc, fs, fr,
               wsem, dsem, xs_s, xs_r, o_s, o_r, ag_s, ag_rz, ag_rp, p_s, p_r, h_s, h_r,
               q_s, q_r, z_s, z_r, f_s, f_r):
        x, z, c = lax.axis_index("dp"), lax.axis_index("tensor"), lax.axis_index("pair")
        ox, oc = 1 - x, 1 - c

        def remote(src, dst, send, recv, **to):
            return pltpu.make_async_remote_copy(
                src_ref=src, dst_ref=dst, send_sem=send, recv_sem=recv, device_id=to, device_id_type=MESH)

        def gu_copies(j, slot):
            col = pl.multiple_of(lax.rem(ox * n_half + j, 2 * n_half) * wide, wide)
            return (pltpu.make_async_copy(gw.at[:, pl.ds(col, wide)], wgb.at[slot, 0], wsem.at[slot, 0]),
                    pltpu.make_async_copy(uw.at[:, pl.ds(col, wide)], wgb.at[slot, 1], wsem.at[slot, 1]))

        def gu_start(j, slot):
            for copy in gu_copies(j, slot):
                copy.start()

        def down_copy(n):
            col = pl.multiple_of(n * span, span)
            return pltpu.make_async_copy(dw.at[:, pl.ds(col, span)], wdb.at[n], dsem.at[n])

        def down_load():
            def step(n, _):
                down_copy(n).start()
                return 0
            lax.fori_loop(0, n_out, step, 0)

        gu_start(0, 0)

        barrier = pltpu.get_barrier_semaphore()
        pl.semaphore_signal(barrier, inc=1, device_id={"dp": ox}, device_id_type=MESH)
        pl.semaphore_signal(barrier, inc=1, device_id={"pair": oc}, device_id_type=MESH)
        for o in range(1, n_z):
            pl.semaphore_signal(barrier, inc=1, device_id={"tensor": lax.rem(z + o, n_z)}, device_id_type=MESH)

        def norm_step(i, _):
            at = pl.ds(pl.multiple_of(i * 16, 16), 16)
            values = tok[at, :].astype(F32)
            inverse = lax.rsqrt(jnp.mean(values * values, axis=1, keepdims=True) + EPSILON)
            kind = kinds[at, 0:1]

            def piece(first):
                cols = pl.ds(pl.multiple_of(first, quarter), quarter)
                chosen = jnp.where(kind == 1, gain[1:2, cols], gain[0:1, cols])
                return (tok[at, cols].astype(F32) * inverse * chosen).astype(BF)

            xs[at, :] = piece(ox * depth + c * quarter)
            place = pl.ds(pl.multiple_of(z * held + i * 16, 16), 16)
            for q in range(2):
                xg[x, q, place, :] = piece(x * depth + q * quarter)
            return 0

        lax.fori_loop(0, held // 16, norm_step, 0)
        pl.semaphore_wait(barrier, n_z + 1)

        def zrows(o):
            return pl.ds(pl.multiple_of(o * held, held), held)

        x_copy = remote(xs, xg.at[x, c, zrows(z)], xs_s, xs_r, dp=ox)
        x_copy.start()
        o_copy = remote(order, order2, o_s, o_r, dp=ox)
        o_copy.start()

        def ag(b, o, way):
            piece = xg.at[b, c, zrows(o)]
            if way == 2:
                return remote(piece, piece, ag_s.at[b, o, 2], ag_rp.at[b, o], pair=oc)
            to = lax.rem(z + (1 if way == 0 else n_z - 1), n_z)
            return remote(piece, piece, ag_s.at[b, o, way], ag_rz.at[b, o], tensor=to)

        def ag_each(b, d, act):
            if d == 0:
                pl.when(z < n_z - 1)(lambda: act(ag(b, z, 0)))
                pl.when(z > 0)(lambda: act(ag(b, z, 1)))
                pl.when(x != b)(lambda: act(ag(b, z, 2)))
                return
            left, right = lax.rem(z - d + n_z, n_z), lax.rem(z + d, n_z)
            pl.when((z >= d) & (z < n_z - 1))(lambda: act(ag(b, left, 0)))
            pl.when(z >= d)(lambda: act(ag(b, left, 2)))
            pl.when((z + d < n_z) & (z > 0))(lambda: act(ag(b, right, 1)))
            pl.when(z + d < n_z)(lambda: act(ag(b, right, 2)))

        def begin(copy):
            copy.start()

        def sent(copy):
            copy.wait_send()

        def own_sends(b):
            @pl.when(x != b)
            def _():
                remote(xs, xg.at[b, c, zrows(z)], xs_s, xs_r, dp=ox).wait_recv()
            ag_each(b, 0, begin)

        def hop(b, d):
            left, right = lax.rem(z - d + n_z, n_z), lax.rem(z + d, n_z)
            pl.when(z >= d)(lambda: ag(b, left, 0).wait_recv())
            pl.when(z + d < n_z)(lambda: ag(b, right, 1).wait_recv())
            ag_each(b, d, begin)

        def sibling(b, o):
            piece = xg.at[b, oc, zrows(o)]
            remote(piece, piece, ag_s.at[b, o, 2], ag_rp.at[b, o], pair=oc).wait_recv()

        def siblings(b, half):
            for k in range(near):
                o = half * near + k
                pl.when((x != b) | (o != z))(lambda: sibling(b, o))

        def p_copy(u, j):
            return remote(ps.at[u, j], pr.at[u, j], p_s.at[u, j], p_r.at[u, j], dp=ox)

        def gate_up(units_of, rows_of, part, final=False):
            def step(j, _):
                slot = lax.rem(j, 2)
                if final:
                    pl.when(j + 1 < 2 * n_half)(lambda: gu_start(j + 1, 1 - slot))
                else:
                    gu_start(lax.rem(j + 1, 2 * n_half), 1 - slot)
                for copy in gu_copies(j, slot):
                    copy.wait()
                for m in range(2):
                    got = (jnp.dot(rows_of(0), wgb[slot, m, :quarter, :], preferred_element_type=F32)
                           + jnp.dot(rows_of(1), wgb[slot, m, quarter:, :], preferred_element_type=F32))
                    for i, u in enumerate(units_of):
                        if part == 0:
                            ps[u, j, m] = got[i * half_rows:(i + 1) * half_rows].astype(BF)
                        else:
                            own[u, j - n_half, m] = got[i * half_rows:(i + 1) * half_rows]
                if part == 0:
                    for u in units_of:
                        p_copy(u, j).start()
                return 0
            lax.fori_loop(part * n_half, (part + 1) * n_half, step, 0)

        def arrived(half):
            at = pl.ds(pl.multiple_of(half * half_rows, half_rows), half_rows)
            return lambda q: xg[0, q, at, :]

        def h_copy(u, j, half):
            piece = hid.at[u, half * n_half + j]
            return remote(piece, piece, h_s.at[u, j], h_r.at[u, j], dp=ox)

        def hidden(u):
            def step(j, _):
                p_copy(u, j).wait_recv()
                gate = own[u, j, 0] + pr[u, j, 0].astype(F32)
                up = own[u, j, 1] + pr[u, j, 1].astype(F32)
                hid[u, x * n_half + j] = (gate / (1.0 + jnp.exp(-gate)) * up).astype(BF)
                h_copy(u, j, x).start()
                return 0
            lax.fori_loop(0, n_half, step, 0)

        def hidden_arrival(u):
            def step(j, _):
                h_copy(u, j, ox).wait_recv()
                return 0
            lax.fori_loop(0, n_half, step, 0)

        def chooser(b):
            at = jnp.where(x == b, order[...], order2[...])[0:1, :]
            match = (lax.broadcasted_iota(jnp.int32, (rows, rows), 0) == at).astype(F32)
            return jnp.transpose(match).astype(BF)

        def sort_hidden():
            chosen = chooser(0)
            for k in range(2 * n_half):
                sh[:, k * wide:(k + 1) * wide] = (
                    jnp.dot(chosen[:, :half_rows], hid[0, k], preferred_element_type=F32)
                    + jnp.dot(chosen[:, half_rows:], hid[1, k], preferred_element_type=F32)).astype(BF)

        def sort_tokens():
            chosen = chooser(1)
            for q in range(2):
                for k in range(0, quarter, span):
                    moved = jnp.dot(chosen, xg[1, q, :, k:k + span], preferred_element_type=F32).astype(BF)
                    xt[q, :, k:k + span] = moved

        def in_order(u):
            for k in range(2 * n_half):
                sh[:half_rows, k * wide:(k + 1) * wide] = hid[u, k]

        def q_copy(u, n):
            return remote(qs.at[u, n], qr.at[u, n], q_s.at[u, n], q_r.at[u, n], pair=oc)

        def z_copy(u, n, o):
            to = lax.rem(z + o, n_z)
            return remote(zs.at[u, n, pl.ds(pl.multiple_of(to * share, share), share)], zr.at[u, n, z],
                          z_s.at[u, n, o], z_r.at[u, n, z], tensor=to)

        def z_arrival(u, n, o):
            src = lax.rem(z + o, n_z)
            return remote(zs.at[u, n, pl.ds(0, share)], zr.at[u, n, src],
                          z_s.at[u, n, o], z_r.at[u, n, src], tensor=src)

        def reduce(units_of, n):
            slot = lax.rem(n, 2)
            for i, u in enumerate(units_of):
                q_copy(u, n).wait_recv()
                total = keep[slot, i] + qr[u, n].astype(F32)
                zs[u, n] = total.astype(BF)
                for o in range(1, n_z):
                    z_copy(u, n, o).start()
                keep[slot, i] = total
                acc[u, n] = keep[slot, i, pl.ds(pl.multiple_of(z * share, share), share), :]

        def down(units_of, loads=False):
            many = len(units_of)

            def step(n, _):
                slot = lax.rem(n, 2)
                if loads:
                    down_copy(n).wait()
                part = jnp.dot(sh[:many * half_rows, :], wdb[n], preferred_element_type=F32)
                for i, u in enumerate(units_of):
                    qs[u, n] = part[i * half_rows + kept:(i + 1) * half_rows].astype(BF)
                    q_copy(u, n).start()
                    keep[slot, i] = part[i * half_rows:i * half_rows + kept]
                pl.when(n >= 1)(lambda: reduce(units_of, n - 1))
                return 0
            lax.fori_loop(0, n_out, step, 0)
            reduce(units_of, n_out - 1)

        def f_copy(h, n):
            return remote(fs.at[h, n], fr.at[h, n], f_s.at[h, n], f_r.at[h, n], dp=ox)

        def finish(u):
            b, h = u // 2, u % 2

            def step(n, _):
                total = acc[u, n]
                for o in range(1, n_z):
                    z_arrival(u, n, o).wait_recv()
                    total = total + zr[u, n, lax.rem(z + o, n_z)].astype(F32)

                @pl.when(x == b)
                def _():
                    out[h * share:(h + 1) * share,
                        pl.ds(pl.multiple_of(b * out_w + n * span, span), span)] = total.astype(BF)

                @pl.when(x != b)
                def _():
                    fs[h, n] = total.astype(BF)
                    f_copy(h, n).start()
                return 0
            lax.fori_loop(0, n_out, step, 0)

        side = z // near
        own_sends(0)
        for d in range(1, near):
            hop(0, d)
        siblings(0, side)
        gate_up((side,), arrived(side), 0)
        hop(0, near)
        gate_up((side,), arrived(side), 1)
        for d in range(near + 1, n_z):
            hop(0, d)
        own_sends(1)
        siblings(0, 1 - side)
        gate_up((1 - side,), arrived(1 - side), 0)
        for d in range(1, near):
            hop(1, d)
        gate_up((1 - side,), arrived(1 - side), 1)
        down_load()
        hop(1, near)
        hidden(side)
        for d in range(near + 1, n_z):
            hop(1, d)
        siblings(1, 0)
        siblings(1, 1)
        o_copy.wait_recv()
        sort_tokens()
        hidden(1 - side)
        gate_up((2, 3), lambda q: xt[q], 0)
        hidden_arrival(0)
        hidden_arrival(1)
        sort_hidden()
        down((0, 1), True)
        gate_up((2, 3), lambda q: xt[q], 1, True)
        hidden(2)
        hidden(3)
        hidden_arrival(2)
        in_order(2)
        down((2,))
        hidden_arrival(3)
        in_order(3)
        down((3,))
        for u in range(4):
            finish(u)

        for h in range(2):
            def last(n, _):
                f_copy(h, n).wait_recv()
                out[h * share:(h + 1) * share,
                    pl.ds(pl.multiple_of(ox * out_w + n * span, span), span)] = fr[h, n]
                return 0
            lax.fori_loop(0, n_out, last, 0)

        x_copy.wait_send()
        o_copy.wait_send()
        for b in range(2):
            for d in range(n_z):
                ag_each(b, d, sent)

        def sent_unit(u, _):
            def sent_x(j, _):
                p_copy(u, j).wait_send()
                h_copy(u, j, x).wait_send()
                return 0
            lax.fori_loop(0, n_half, sent_x, 0)

            def sent_z(n, _):
                q_copy(u, n).wait_send()
                for o in range(1, n_z):
                    z_copy(u, n, o).wait_send()
                return 0
            lax.fori_loop(0, n_out, sent_z, 0)
            return 0
        lax.fori_loop(0, 4, sent_unit, 0)

        def sent_f(n, _):
            f_copy(0, n).wait_send()
            f_copy(1, n).wait_send()
            return 0
        lax.fori_loop(0, n_out, sent_f, 0)

    z, c = lax.axis_index("tensor"), lax.axis_index("pair")
    kinds = lax.dynamic_slice_in_dim(modality, z * held, held, 0)
    kinds = jnp.broadcast_to(kinds[:, None], (held, 128))
    order = time_order.reshape(n_z, 2, 2, share).transpose(2, 1, 0, 3)
    order = jnp.where(c == 0, order, order[:, ::-1]).reshape(1, rows)
    order = jnp.broadcast_to(order, (8, rows))
    vmem, anywhere = pl.BlockSpec(memory_space=pltpu.VMEM), pl.BlockSpec(memory_space=pl.ANY)
    dma = pltpu.SemaphoreType.DMA
    scratch = [
        pltpu.VMEM((held, quarter), BF),
        pltpu.VMEM((2, 2, rows, quarter), BF),
        pltpu.VMEM((2, rows, quarter), BF),
        pltpu.VMEM((8, rows), jnp.int32),
        pltpu.VMEM((2, 2, depth, wide), BF),
        pltpu.VMEM((n_out, units, span), BF),
        pltpu.VMEM((4, n_half, 2, half_rows, wide), BF),
        pltpu.VMEM((4, n_half, 2, half_rows, wide), BF),
        pltpu.VMEM((4, n_half, 2, half_rows, wide), F32),
        pltpu.VMEM((4, 2 * n_half, half_rows, wide), BF),
        pltpu.VMEM((rows, units), BF),
        pltpu.VMEM((4, n_out, kept, span), BF),
        pltpu.VMEM((4, n_out, kept, span), BF),
        pltpu.VMEM((2, 2, kept, span), F32),
        pltpu.VMEM((4, n_out, kept, span), BF),
        pltpu.VMEM((4, n_out, n_z, share, span), BF),
        pltpu.VMEM((4, n_out, share, span), F32),
        pltpu.VMEM((2, n_out, share, span), BF),
        pltpu.VMEM((2, n_out, share, span), BF),
        dma((2, 2)), dma((n_out,)), dma, dma, dma, dma,
        dma((2, n_z, 3)), dma((2, n_z)), dma((2, n_z)),
        dma((4, n_half)), dma((4, n_half)), dma((4, n_half)), dma((4, n_half)),
        dma((4, n_out)), dma((4, n_out)), dma((4, n_out, n_z)), dma((4, n_out, n_z)),
        dma((2, n_out)), dma((2, n_out)),
    ]
    return pl.pallas_call(
        kernel,
        out_shape=jax.ShapeDtypeStruct((rows // (n_z * 2), width), BF),
        in_specs=[vmem, vmem, vmem, vmem, anywhere, anywhere, anywhere],
        out_specs=vmem,
        scratch_shapes=scratch,
        compiler_params=pltpu.CompilerParams(
            collective_id=0, has_side_effects=True, vmem_limit_bytes=60 * 2**20),
        cost_estimate=pl.CostEstimate(
            flops=12 * rows * depth * units, bytes_accessed=12 * depth * units, transcendentals=0),
    )(tokens, kinds, order, norm_gain, gate_weight, up_weight, down_weight)


def solution(mesh):
    placed = (
        P(("groups", "dp", "tensor"), None),
        P(("groups", "dp")),
        P(("groups", "dp")),
        P(),
        P("dp", ("tensor", "pair")),
        P("dp", ("tensor", "pair")),
        P(("tensor", "pair"), "dp"),
    )

    def per_device(*arrays):
        share = arrays[1].shape[0] // (mesh.shape["tensor"] * mesh.shape["pair"])
        if mesh.shape["dp"] == 2 and mesh.shape["pair"] == 2 and share % 32 == 0:
            return fused(mesh, *arrays)
        return plain(mesh, *arrays)

    return jax.shard_map(
        per_device,
        mesh=mesh,
        in_specs=placed,
        out_specs=P(("groups", "dp", "tensor", "pair"), None),
        check_vma=False,
    )
```

```python
import jax
import jax.numpy as jnp
from jax import lax
from jax.experimental import pallas as pl
from jax.experimental.pallas import tpu as pltpu
from jax.sharding import PartitionSpec as P

EPSILON = 1e-05
BF, F32 = jnp.bfloat16, jnp.float32
MESH = pl.DeviceIdType.MESH


def normalize(block_rows, row_kinds, norm_gain):
    values = block_rows.astype(jnp.float32)
    inverse_rms = lax.rsqrt(jnp.mean(values * values, axis=1, keepdims=True) + EPSILON)
    chosen = jnp.where(row_kinds[:, None] == 1, norm_gain[1][None, :], norm_gain[0][None, :])
    return (values * inverse_rms * chosen).astype(jnp.bfloat16)


def exchange(pieces, n_dp):
    me = lax.axis_index("dp")
    got = jnp.zeros_like(pieces)
    got = lax.dynamic_update_index_in_dim(got, lax.dynamic_index_in_dim(pieces, me, 0, False), me, 0)
    for shift in range(1, n_dp):
        to = lax.rem(me + shift, n_dp)
        arrived = lax.ppermute(
            lax.dynamic_index_in_dim(pieces, to, 0, False),
            "dp",
            [(i, (i + shift) % n_dp) for i in range(n_dp)],
        )
        got = lax.dynamic_update_index_in_dim(got, arrived, lax.rem(me - shift + n_dp, n_dp), 0)
    return got


def spread(block, n_dp):
    me = lax.axis_index("dp")
    got = jnp.zeros((n_dp,) + block.shape, block.dtype)
    got = lax.dynamic_update_index_in_dim(got, block, me, 0)
    for shift in range(1, n_dp):
        arrived = lax.ppermute(block, "dp", [(i, (i + shift) % n_dp) for i in range(n_dp)])
        got = lax.dynamic_update_index_in_dim(got, arrived, lax.rem(me - shift + n_dp, n_dp), 0)
    return got


def plain(mesh, tokens, time_order, modality, norm_gain, gate_weight, up_weight, down_weight):
    n_dp, n_tensor, n_pair = mesh.shape["dp"], mesh.shape["tensor"], mesh.shape["pair"]
    held, width = tokens.shape
    rows = time_order.shape[0]
    depth, hidden_units = gate_weight.shape
    first = lax.axis_index("tensor") * held
    normed = normalize(tokens, lax.dynamic_slice_in_dim(modality, first, held, 0), norm_gain)
    by_part = normed.reshape(held, n_dp, depth).transpose(1, 0, 2)
    blocks = exchange(by_part, n_dp)
    every = lax.all_gather(blocks, "tensor", axis=1, tiled=True).reshape(n_dp * rows, depth)
    gate_part = jnp.dot(every, gate_weight, preferred_element_type=jnp.float32)
    up_part = jnp.dot(every, up_weight, preferred_element_type=jnp.float32)
    both = jnp.stack([gate_part, up_part]).reshape(2, n_dp, rows, hidden_units).transpose(1, 0, 2, 3)
    got = exchange(both.astype(jnp.bfloat16), n_dp).astype(jnp.float32)
    own = lax.axis_index("dp")
    mine = lax.dynamic_index_in_dim(both, own, 0, False)
    at = jnp.arange(n_dp)[:, None, None, None]
    summed = mine + jnp.sum(jnp.where(at == own, 0.0, got), axis=0)
    hidden = (jax.nn.silu(summed[0]) * summed[1]).astype(jnp.bfloat16)
    chosen = (time_order[:, None] == jnp.arange(rows)[None, :]).astype(jnp.bfloat16)
    hidden = jnp.dot(chosen, hidden, preferred_element_type=jnp.float32).astype(jnp.bfloat16)
    hidden = spread(hidden, n_dp).reshape(n_dp * rows, hidden_units)
    partial = jnp.dot(hidden, down_weight, preferred_element_type=jnp.float32).astype(jnp.bfloat16)
    partial = partial.reshape(n_dp, rows, -1)
    partial = lax.psum_scatter(partial, ("tensor", "pair"), scatter_dimension=1, tiled=True)
    return exchange(partial, n_dp).transpose(1, 0, 2).reshape(rows // (n_tensor * n_pair), width)


def fused(mesh, tokens, time_order, modality, norm_gain, gate_weight, up_weight, down_weight):
    n_z = mesh.shape["tensor"]
    held, width = tokens.shape
    rows = time_order.shape[0]
    depth, units = gate_weight.shape
    out_w = down_weight.shape[1]
    quarter = depth // 2
    wide = 256
    n_half = units // 2 // wide
    span = 512
    n_out = out_w // span
    half_rows = rows // 2
    near = n_z // 2
    kept = half_rows // 2
    share = kept // n_z

    def kernel(tok, kinds, order, gain, gw, uw, dw, out,
               xs, xg, xt, order2, wgb, wdb, ps, pr, own, hid, sh, qs, qr, keep, zs, zr, zs2, zr2, acc, fs, fr,
               wsem, dsem, xs_s, xs_r, o_s, o_r, ag_s, ag_rz, ag_rp, p_s, p_r, h_s, h_r,
               q_s, q_r, n_s, n_r, z_s, z_r, f_s, f_r):
        x, z, c = lax.axis_index("dp"), lax.axis_index("tensor"), lax.axis_index("pair")
        ox, oc = 1 - x, 1 - c

        def remote(src, dst, send, recv, **to):
            return pltpu.make_async_remote_copy(
                src_ref=src, dst_ref=dst, send_sem=send, recv_sem=recv, device_id=to, device_id_type=MESH)

        def gu_copies(j, slot):
            col = pl.multiple_of(lax.rem(ox * n_half + j, 2 * n_half) * wide, wide)
            return (pltpu.make_async_copy(gw.at[:, pl.ds(col, wide)], wgb.at[slot, 0], wsem.at[slot, 0]),
                    pltpu.make_async_copy(uw.at[:, pl.ds(col, wide)], wgb.at[slot, 1], wsem.at[slot, 1]))

        def gu_start(j, slot):
            for copy in gu_copies(j, slot):
                copy.start()

        def down_copy(n):
            col = pl.multiple_of(n * span, span)
            return pltpu.make_async_copy(dw.at[:, pl.ds(col, span)], wdb.at[n], dsem.at[n])

        def down_load():
            def step(n, _):
                down_copy(n).start()
                return 0
            lax.fori_loop(0, n_out, step, 0)

        gu_start(0, 0)

        barrier = pltpu.get_barrier_semaphore()
        pl.semaphore_signal(barrier, inc=1, device_id={"dp": ox}, device_id_type=MESH)
        pl.semaphore_signal(barrier, inc=1, device_id={"pair": oc}, device_id_type=MESH)
        for o in range(1, n_z):
            pl.semaphore_signal(barrier, inc=1, device_id={"tensor": lax.rem(z + o, n_z)}, device_id_type=MESH)

        def norm_step(i, _):
            at = pl.ds(pl.multiple_of(i * 16, 16), 16)
            values = tok[at, :].astype(F32)
            inverse = lax.rsqrt(jnp.mean(values * values, axis=1, keepdims=True) + EPSILON)
            kind = kinds[at, 0:1]

            def piece(first):
                cols = pl.ds(pl.multiple_of(first, quarter), quarter)
                chosen = jnp.where(kind == 1, gain[1:2, cols], gain[0:1, cols])
                return (tok[at, cols].astype(F32) * inverse * chosen).astype(BF)

            xs[at, :] = piece(ox * depth + c * quarter)
            place = pl.ds(pl.multiple_of(z * held + i * 16, 16), 16)
            for q in range(2):
                xg[x, q, place, :] = piece(x * depth + q * quarter)
            return 0

        lax.fori_loop(0, held // 16, norm_step, 0)
        pl.semaphore_wait(barrier, n_z + 1)

        def zrows(o):
            return pl.ds(pl.multiple_of(o * held, held), held)

        x_copy = remote(xs, xg.at[x, c, zrows(z)], xs_s, xs_r, dp=ox)
        x_copy.start()
        o_copy = remote(order, order2, o_s, o_r, dp=ox)
        o_copy.start()

        def ag(b, o, way):
            piece = xg.at[b, c, zrows(o)]
            if way == 2:
                return remote(piece, piece, ag_s.at[b, o, 2], ag_rp.at[b, o], pair=oc)
            to = lax.rem(z + (1 if way == 0 else n_z - 1), n_z)
            return remote(piece, piece, ag_s.at[b, o, way], ag_rz.at[b, o], tensor=to)

        def ag_each(b, d, act):
            if d == 0:
                pl.when(z < n_z - 1)(lambda: act(ag(b, z, 0)))
                pl.when(z > 0)(lambda: act(ag(b, z, 1)))
                pl.when(x != b)(lambda: act(ag(b, z, 2)))
                return
            left, right = lax.rem(z - d + n_z, n_z), lax.rem(z + d, n_z)
            pl.when((z >= d) & (z < n_z - 1))(lambda: act(ag(b, left, 0)))
            pl.when(z >= d)(lambda: act(ag(b, left, 2)))
            pl.when((z + d < n_z) & (z > 0))(lambda: act(ag(b, right, 1)))
            pl.when(z + d < n_z)(lambda: act(ag(b, right, 2)))

        def begin(copy):
            copy.start()

        def sent(copy):
            copy.wait_send()

        def own_sends(b):
            @pl.when(x != b)
            def _():
                remote(xs, xg.at[b, c, zrows(z)], xs_s, xs_r, dp=ox).wait_recv()
            ag_each(b, 0, begin)

        def hop(b, d):
            left, right = lax.rem(z - d + n_z, n_z), lax.rem(z + d, n_z)
            pl.when(z >= d)(lambda: ag(b, left, 0).wait_recv())
            pl.when(z + d < n_z)(lambda: ag(b, right, 1).wait_recv())
            ag_each(b, d, begin)

        def sibling(b, o):
            piece = xg.at[b, oc, zrows(o)]
            remote(piece, piece, ag_s.at[b, o, 2], ag_rp.at[b, o], pair=oc).wait_recv()

        def siblings(b, half):
            for k in range(near):
                o = half * near + k
                pl.when((x != b) | (o != z))(lambda: sibling(b, o))

        def p_copy(u, j):
            return remote(ps.at[u, j], pr.at[u, j], p_s.at[u, j], p_r.at[u, j], dp=ox)

        def gate_up(units_of, rows_of, part, final=False):
            def step(j, _):
                slot = lax.rem(j, 2)
                if final:
                    pl.when(j + 1 < 2 * n_half)(lambda: gu_start(j + 1, 1 - slot))
                else:
                    gu_start(lax.rem(j + 1, 2 * n_half), 1 - slot)
                for copy in gu_copies(j, slot):
                    copy.wait()
                for m in range(2):
                    got = (jnp.dot(rows_of(0), wgb[slot, m, :quarter, :], preferred_element_type=F32)
                           + jnp.dot(rows_of(1), wgb[slot, m, quarter:, :], preferred_element_type=F32))
                    for i, u in enumerate(units_of):
                        if part == 0:
                            ps[u, j, m] = got[i * half_rows:(i + 1) * half_rows].astype(BF)
                        else:
                            own[u, j - n_half, m] = got[i * half_rows:(i + 1) * half_rows]
                if part == 0:
                    for u in units_of:
                        p_copy(u, j).start()
                return 0
            lax.fori_loop(part * n_half, (part + 1) * n_half, step, 0)

        def arrived(half):
            at = pl.ds(pl.multiple_of(half * half_rows, half_rows), half_rows)
            return lambda q: xg[0, q, at, :]

        def h_copy(u, j, half):
            piece = hid.at[u, half * n_half + j]
            return remote(piece, piece, h_s.at[u, j], h_r.at[u, j], dp=ox)

        def hidden(u):
            def step(j, _):
                p_copy(u, j).wait_recv()
                gate = own[u, j, 0] + pr[u, j, 0].astype(F32)
                up = own[u, j, 1] + pr[u, j, 1].astype(F32)
                hid[u, x * n_half + j] = (gate / (1.0 + jnp.exp(-gate)) * up).astype(BF)
                h_copy(u, j, x).start()
                return 0
            lax.fori_loop(0, n_half, step, 0)

        def hidden_arrival(u):
            def step(j, _):
                h_copy(u, j, ox).wait_recv()
                return 0
            lax.fori_loop(0, n_half, step, 0)

        def chooser(b):
            at = jnp.where(x == b, order[...], order2[...])[0:1, :]
            match = (lax.broadcasted_iota(jnp.int32, (rows, rows), 0) == at).astype(F32)
            return jnp.transpose(match).astype(BF)

        def sort_hidden():
            chosen = chooser(0)
            for k in range(2 * n_half):
                sh[:, k * wide:(k + 1) * wide] = (
                    jnp.dot(chosen[:, :half_rows], hid[0, k], preferred_element_type=F32)
                    + jnp.dot(chosen[:, half_rows:], hid[1, k], preferred_element_type=F32)).astype(BF)

        def sort_tokens():
            chosen = chooser(1)
            for q in range(2):
                for k in range(0, quarter, span):
                    moved = jnp.dot(chosen, xg[1, q, :, k:k + span], preferred_element_type=F32).astype(BF)
                    xt[q, :, k:k + span] = moved

        def in_order(u):
            for k in range(2 * n_half):
                sh[:half_rows, k * wide:(k + 1) * wide] = hid[u, k]

        def q_copy(u, n):
            return remote(qs.at[u, n], qr.at[u, n], q_s.at[u, n], q_r.at[u, n], pair=oc)

        low, high = lax.rem(z, 2), z // 2

        def near_copy(u, n):
            mine = zs.at[u, n, pl.ds(pl.multiple_of((1 - low) * 2 * share, 2 * share), 2 * share)]
            return remote(mine, zr.at[u, n], n_s.at[u, n], n_r.at[u, n], tensor=z + 1 - 2 * low)

        def far_copy(u, n):
            mine = zs2.at[u, n, pl.ds(pl.multiple_of((1 - high) * share, share), share)]
            return remote(mine, zr2.at[u, n], z_s.at[u, n], z_r.at[u, n], tensor=lax.rem(z + 2, n_z))

        def reduce(units_of, n):
            slot = lax.rem(n, 2)
            for i, u in enumerate(units_of):
                q_copy(u, n).wait_recv()
                total = keep[slot, i] + qr[u, n].astype(F32)
                zs[u, n] = total.astype(BF)
                near_copy(u, n).start()
                keep[slot, i] = total
                acc[u, n] = keep[slot, i, pl.ds(pl.multiple_of(low * 2 * share, 2 * share), 2 * share), :]

        def relay(u, n):
            near_copy(u, n).wait_recv()
            total = acc[u, n] + zr[u, n].astype(F32)
            acc[u, n] = total
            zs2[u, n] = total.astype(BF)
            far_copy(u, n).start()

        def relays(u):
            def step(n, _):
                relay(u, n)
                return 0
            lax.fori_loop(0, n_out, step, 0)

        def down(units_of, loads=False, passing=None):
            many = len(units_of)

            def step(n, _):
                slot = lax.rem(n, 2)
                if loads:
                    down_copy(n).wait()
                part = jnp.dot(sh[:many * half_rows, :], wdb[n], preferred_element_type=F32)
                for i, u in enumerate(units_of):
                    qs[u, n] = part[i * half_rows + kept:(i + 1) * half_rows].astype(BF)
                    q_copy(u, n).start()
                    keep[slot, i] = part[i * half_rows:i * half_rows + kept]
                pl.when(n >= 1)(lambda: reduce(units_of, n - 1))
                if passing is not None:
                    relay(passing, n)
                return 0
            lax.fori_loop(0, n_out, step, 0)
            reduce(units_of, n_out - 1)

        def f_copy(h, n):
            return remote(fs.at[h, n], fr.at[h, n], f_s.at[h, n], f_r.at[h, n], dp=ox)

        def finish(u):
            b, h = u // 2, u % 2

            def step(n, _):
                far_copy(u, n).wait_recv()
                total = acc[u, n, pl.ds(pl.multiple_of(high * share, share), share), :] + zr2[u, n].astype(F32)

                @pl.when(x == b)
                def _():
                    out[h * share:(h + 1) * share,
                        pl.ds(pl.multiple_of(b * out_w + n * span, span), span)] = total.astype(BF)

                @pl.when(x != b)
                def _():
                    fs[h, n] = total.astype(BF)
                    f_copy(h, n).start()
                return 0
            lax.fori_loop(0, n_out, step, 0)

        side = z // near
        own_sends(0)
        for d in range(1, near):
            hop(0, d)
        siblings(0, side)
        gate_up((side,), arrived(side), 0)
        hop(0, near)
        gate_up((side,), arrived(side), 1)
        for d in range(near + 1, n_z):
            hop(0, d)
        own_sends(1)
        siblings(0, 1 - side)
        gate_up((1 - side,), arrived(1 - side), 0)
        for d in range(1, near):
            hop(1, d)
        gate_up((1 - side,), arrived(1 - side), 1)
        down_load()
        hop(1, near)
        hidden(side)
        for d in range(near + 1, n_z):
            hop(1, d)
        siblings(1, 0)
        siblings(1, 1)
        o_copy.wait_recv()
        sort_tokens()
        hidden(1 - side)
        gate_up((2, 3), lambda q: xt[q], 0)
        hidden_arrival(0)
        hidden_arrival(1)
        sort_hidden()
        down((0, 1), True)
        gate_up((2, 3), lambda q: xt[q], 1, True)
        hidden(2)
        hidden(3)
        relays(0)
        relays(1)
        hidden_arrival(2)
        in_order(2)
        down((2,))
        hidden_arrival(3)
        in_order(3)
        down((3,), passing=2)
        finish(0)
        finish(1)
        relays(3)
        finish(2)
        finish(3)

        for h in range(2):
            def last(n, _):
                f_copy(h, n).wait_recv()
                out[h * share:(h + 1) * share,
                    pl.ds(pl.multiple_of(ox * out_w + n * span, span), span)] = fr[h, n]
                return 0
            lax.fori_loop(0, n_out, last, 0)

        x_copy.wait_send()
        o_copy.wait_send()
        for b in range(2):
            for d in range(n_z):
                ag_each(b, d, sent)

        def sent_unit(u, _):
            def sent_x(j, _):
                p_copy(u, j).wait_send()
                h_copy(u, j, x).wait_send()
                return 0
            lax.fori_loop(0, n_half, sent_x, 0)

            def sent_z(n, _):
                q_copy(u, n).wait_send()
                near_copy(u, n).wait_send()
                far_copy(u, n).wait_send()
                return 0
            lax.fori_loop(0, n_out, sent_z, 0)
            return 0
        lax.fori_loop(0, 4, sent_unit, 0)

        def sent_f(n, _):
            f_copy(0, n).wait_send()
            f_copy(1, n).wait_send()
            return 0
        lax.fori_loop(0, n_out, sent_f, 0)

    z, c = lax.axis_index("tensor"), lax.axis_index("pair")
    kinds = lax.dynamic_slice_in_dim(modality, z * held, held, 0)
    kinds = jnp.broadcast_to(kinds[:, None], (held, 128))
    order = time_order.reshape(2, 2, 2, 2, share).transpose(3, 2, 1, 0, 4)
    order = jnp.where(c == 0, order, order[:, ::-1]).reshape(1, rows)
    order = jnp.broadcast_to(order, (8, rows))
    vmem, anywhere = pl.BlockSpec(memory_space=pltpu.VMEM), pl.BlockSpec(memory_space=pl.ANY)
    dma = pltpu.SemaphoreType.DMA
    scratch = [
        pltpu.VMEM((held, quarter), BF),
        pltpu.VMEM((2, 2, rows, quarter), BF),
        pltpu.VMEM((2, rows, quarter), BF),
        pltpu.VMEM((8, rows), jnp.int32),
        pltpu.VMEM((2, 2, depth, wide), BF),
        pltpu.VMEM((n_out, units, span), BF),
        pltpu.VMEM((4, n_half, 2, half_rows, wide), BF),
        pltpu.VMEM((4, n_half, 2, half_rows, wide), BF),
        pltpu.VMEM((4, n_half, 2, half_rows, wide), F32),
        pltpu.VMEM((4, 2 * n_half, half_rows, wide), BF),
        pltpu.VMEM((rows, units), BF),
        pltpu.VMEM((4, n_out, kept, span), BF),
        pltpu.VMEM((4, n_out, kept, span), BF),
        pltpu.VMEM((2, 2, kept, span), F32),
        pltpu.VMEM((4, n_out, kept, span), BF),
        pltpu.VMEM((4, n_out, 2 * share, span), BF),
        pltpu.VMEM((4, n_out, 2 * share, span), BF),
        pltpu.VMEM((4, n_out, share, span), BF),
        pltpu.VMEM((4, n_out, 2 * share, span), F32),
        pltpu.VMEM((2, n_out, share, span), BF),
        pltpu.VMEM((2, n_out, share, span), BF),
        dma((2, 2)), dma((n_out,)), dma, dma, dma, dma,
        dma((2, n_z, 3)), dma((2, n_z)), dma((2, n_z)),
        dma((4, n_half)), dma((4, n_half)), dma((4, n_half)), dma((4, n_half)),
        dma((4, n_out)), dma((4, n_out)), dma((4, n_out)), dma((4, n_out)), dma((4, n_out)), dma((4, n_out)),
        dma((2, n_out)), dma((2, n_out)),
    ]
    return pl.pallas_call(
        kernel,
        out_shape=jax.ShapeDtypeStruct((rows // (n_z * 2), width), BF),
        in_specs=[vmem, vmem, vmem, vmem, anywhere, anywhere, anywhere],
        out_specs=vmem,
        scratch_shapes=scratch,
        compiler_params=pltpu.CompilerParams(
            collective_id=0, has_side_effects=True, vmem_limit_bytes=60 * 2**20),
        cost_estimate=pl.CostEstimate(
            flops=12 * rows * depth * units, bytes_accessed=12 * depth * units, transcendentals=0),
    )(tokens, kinds, order, norm_gain, gate_weight, up_weight, down_weight)


def solution(mesh):
    placed = (
        P(("groups", "dp", "tensor"), None),
        P(("groups", "dp")),
        P(("groups", "dp")),
        P(),
        P("dp", ("tensor", "pair")),
        P("dp", ("tensor", "pair")),
        P(("tensor", "pair"), "dp"),
    )

    def per_device(*arrays):
        share = arrays[1].shape[0] // (mesh.shape["tensor"] * mesh.shape["pair"])
        if mesh.shape["dp"] == 2 and mesh.shape["pair"] == 2 and mesh.shape["tensor"] == 4 and share % 32 == 0:
            return fused(mesh, *arrays)
        return plain(mesh, *arrays)

    return jax.shard_map(
        per_device,
        mesh=mesh,
        in_specs=placed,
        out_specs=P(("groups", "dp", "tensor", "pair"), None),
        check_vma=False,
    )
```

```python
import jax
import jax.numpy as jnp
from jax import lax
from jax.experimental import pallas as pl
from jax.experimental.pallas import tpu as pltpu
from jax.sharding import PartitionSpec as P

EPSILON = 1e-05
BF, F32 = jnp.bfloat16, jnp.float32
MESH = pl.DeviceIdType.MESH


def normalize(block_rows, row_kinds, norm_gain):
    values = block_rows.astype(jnp.float32)
    inverse_rms = lax.rsqrt(jnp.mean(values * values, axis=1, keepdims=True) + EPSILON)
    chosen = jnp.where(row_kinds[:, None] == 1, norm_gain[1][None, :], norm_gain[0][None, :])
    return (values * inverse_rms * chosen).astype(jnp.bfloat16)


def exchange(pieces, n_dp):
    me = lax.axis_index("dp")
    got = jnp.zeros_like(pieces)
    got = lax.dynamic_update_index_in_dim(got, lax.dynamic_index_in_dim(pieces, me, 0, False), me, 0)
    for shift in range(1, n_dp):
        to = lax.rem(me + shift, n_dp)
        arrived = lax.ppermute(
            lax.dynamic_index_in_dim(pieces, to, 0, False),
            "dp",
            [(i, (i + shift) % n_dp) for i in range(n_dp)],
        )
        got = lax.dynamic_update_index_in_dim(got, arrived, lax.rem(me - shift + n_dp, n_dp), 0)
    return got


def spread(block, n_dp):
    me = lax.axis_index("dp")
    got = jnp.zeros((n_dp,) + block.shape, block.dtype)
    got = lax.dynamic_update_index_in_dim(got, block, me, 0)
    for shift in range(1, n_dp):
        arrived = lax.ppermute(block, "dp", [(i, (i + shift) % n_dp) for i in range(n_dp)])
        got = lax.dynamic_update_index_in_dim(got, arrived, lax.rem(me - shift + n_dp, n_dp), 0)
    return got


def plain(mesh, tokens, time_order, modality, norm_gain, gate_weight, up_weight, down_weight):
    n_dp, n_tensor, n_pair = mesh.shape["dp"], mesh.shape["tensor"], mesh.shape["pair"]
    held, width = tokens.shape
    rows = time_order.shape[0]
    depth, hidden_units = gate_weight.shape
    first = lax.axis_index("tensor") * held
    normed = normalize(tokens, lax.dynamic_slice_in_dim(modality, first, held, 0), norm_gain)
    by_part = normed.reshape(held, n_dp, depth).transpose(1, 0, 2)
    blocks = exchange(by_part, n_dp)
    every = lax.all_gather(blocks, "tensor", axis=1, tiled=True).reshape(n_dp * rows, depth)
    gate_part = jnp.dot(every, gate_weight, preferred_element_type=jnp.float32)
    up_part = jnp.dot(every, up_weight, preferred_element_type=jnp.float32)
    both = jnp.stack([gate_part, up_part]).reshape(2, n_dp, rows, hidden_units).transpose(1, 0, 2, 3)
    got = exchange(both.astype(jnp.bfloat16), n_dp).astype(jnp.float32)
    own = lax.axis_index("dp")
    mine = lax.dynamic_index_in_dim(both, own, 0, False)
    at = jnp.arange(n_dp)[:, None, None, None]
    summed = mine + jnp.sum(jnp.where(at == own, 0.0, got), axis=0)
    hidden = (jax.nn.silu(summed[0]) * summed[1]).astype(jnp.bfloat16)
    chosen = (time_order[:, None] == jnp.arange(rows)[None, :]).astype(jnp.bfloat16)
    hidden = jnp.dot(chosen, hidden, preferred_element_type=jnp.float32).astype(jnp.bfloat16)
    hidden = spread(hidden, n_dp).reshape(n_dp * rows, hidden_units)
    partial = jnp.dot(hidden, down_weight, preferred_element_type=jnp.float32).astype(jnp.bfloat16)
    partial = partial.reshape(n_dp, rows, -1)
    partial = lax.psum_scatter(partial, ("tensor", "pair"), scatter_dimension=1, tiled=True)
    return exchange(partial, n_dp).transpose(1, 0, 2).reshape(rows // (n_tensor * n_pair), width)


def fused(mesh, tokens, time_order, modality, norm_gain, gate_weight, up_weight, down_weight):
    n_z = mesh.shape["tensor"]
    held, width = tokens.shape
    rows = time_order.shape[0]
    depth, units = gate_weight.shape
    out_w = down_weight.shape[1]
    quarter = depth // 2
    wide = 256
    n_half = units // 2 // wide
    span = 512
    n_out = out_w // span
    half_rows = rows // 2
    near = n_z // 2
    kept = half_rows // 2
    share = kept // n_z

    def kernel(tok, kinds, order, gain, gw, uw, dw, out,
               xs, xg, xt, order2, wgb, wdb, ps, pr, own, hid, sh, qs, qr, keep, zs, zr, zs2, zr2, acc, fs, fr,
               wsem, dsem, xs_s, xs_r, o_s, o_r, ag_s, ag_rz, ag_rp, p_s, p_r, h_s, h_r,
               q_s, q_r, n_s, n_r, z_s, z_r, f_s, f_r):
        x, z, c = lax.axis_index("dp"), lax.axis_index("tensor"), lax.axis_index("pair")
        ox, oc = 1 - x, 1 - c

        def remote(src, dst, send, recv, **to):
            return pltpu.make_async_remote_copy(
                src_ref=src, dst_ref=dst, send_sem=send, recv_sem=recv, device_id=to, device_id_type=MESH)

        def gu_copies(j, slot):
            col = pl.multiple_of(lax.rem(ox * n_half + j, 2 * n_half) * wide, wide)
            return (pltpu.make_async_copy(gw.at[:, pl.ds(col, wide)], wgb.at[slot, 0], wsem.at[slot, 0]),
                    pltpu.make_async_copy(uw.at[:, pl.ds(col, wide)], wgb.at[slot, 1], wsem.at[slot, 1]))

        def gu_start(j, slot):
            for copy in gu_copies(j, slot):
                copy.start()

        def down_copy(n):
            col = pl.multiple_of(n * span, span)
            return pltpu.make_async_copy(dw.at[:, pl.ds(col, span)], wdb.at[n], dsem.at[n])

        def down_load():
            def step(n, _):
                down_copy(n).start()
                return 0
            lax.fori_loop(0, n_out, step, 0)

        gu_start(0, 0)

        barrier = pltpu.get_barrier_semaphore()
        pl.semaphore_signal(barrier, inc=1, device_id={"dp": ox}, device_id_type=MESH)
        pl.semaphore_signal(barrier, inc=1, device_id={"pair": oc}, device_id_type=MESH)
        for o in range(1, n_z):
            pl.semaphore_signal(barrier, inc=1, device_id={"tensor": lax.rem(z + o, n_z)}, device_id_type=MESH)

        def norm_step(i, _):
            at = pl.ds(pl.multiple_of(i * 16, 16), 16)
            values = tok[at, :].astype(F32)
            inverse = lax.rsqrt(jnp.mean(values * values, axis=1, keepdims=True) + EPSILON)
            kind = kinds[at, 0:1]

            def piece(first):
                cols = pl.ds(pl.multiple_of(first, quarter), quarter)
                chosen = jnp.where(kind == 1, gain[1:2, cols], gain[0:1, cols])
                return (tok[at, cols].astype(F32) * inverse * chosen).astype(BF)

            xs[at, :] = piece(ox * depth + c * quarter)
            place = pl.ds(pl.multiple_of(z * held + i * 16, 16), 16)
            for q in range(2):
                xg[x, q, place, :] = piece(x * depth + q * quarter)
            return 0

        lax.fori_loop(0, held // 16, norm_step, 0)
        pl.semaphore_wait(barrier, n_z + 1)

        def zrows(o):
            return pl.ds(pl.multiple_of(o * held, held), held)

        x_copy = remote(xs, xg.at[x, c, zrows(z)], xs_s, xs_r, dp=ox)
        x_copy.start()
        o_copy = remote(order, order2, o_s, o_r, dp=ox)
        o_copy.start()

        def ag(b, o, way):
            piece = xg.at[b, c, zrows(o)]
            if way == 2:
                return remote(piece, piece, ag_s.at[b, o, 2], ag_rp.at[b, o], pair=oc)
            to = lax.rem(z + (1 if way == 0 else n_z - 1), n_z)
            return remote(piece, piece, ag_s.at[b, o, way], ag_rz.at[b, o], tensor=to)

        def ag_each(b, d, act):
            if d == 0:
                pl.when(z < n_z - 1)(lambda: act(ag(b, z, 0)))
                pl.when(z > 0)(lambda: act(ag(b, z, 1)))
                pl.when(x != b)(lambda: act(ag(b, z, 2)))
                return
            left, right = lax.rem(z - d + n_z, n_z), lax.rem(z + d, n_z)
            pl.when((z >= d) & (z < n_z - 1))(lambda: act(ag(b, left, 0)))
            pl.when(z >= d)(lambda: act(ag(b, left, 2)))
            pl.when((z + d < n_z) & (z > 0))(lambda: act(ag(b, right, 1)))
            pl.when(z + d < n_z)(lambda: act(ag(b, right, 2)))

        def begin(copy):
            copy.start()

        def sent(copy):
            copy.wait_send()

        def own_sends(b):
            @pl.when(x != b)
            def _():
                remote(xs, xg.at[b, c, zrows(z)], xs_s, xs_r, dp=ox).wait_recv()
            ag_each(b, 0, begin)

        def hop(b, d):
            left, right = lax.rem(z - d + n_z, n_z), lax.rem(z + d, n_z)
            pl.when(z >= d)(lambda: ag(b, left, 0).wait_recv())
            pl.when(z + d < n_z)(lambda: ag(b, right, 1).wait_recv())
            ag_each(b, d, begin)

        def sibling(b, o):
            piece = xg.at[b, oc, zrows(o)]
            remote(piece, piece, ag_s.at[b, o, 2], ag_rp.at[b, o], pair=oc).wait_recv()

        def siblings(b, half):
            for k in range(near):
                o = half * near + k
                pl.when((x != b) | (o != z))(lambda: sibling(b, o))

        def p_copy(u, j):
            return remote(ps.at[u, j], pr.at[u, j], p_s.at[u, j], p_r.at[u, j], dp=ox)

        def gate_up(units_of, rows_of, part, final=False):
            def step(j, _):
                slot = lax.rem(j, 2)
                if final:
                    pl.when(j + 1 < 2 * n_half)(lambda: gu_start(j + 1, 1 - slot))
                else:
                    gu_start(lax.rem(j + 1, 2 * n_half), 1 - slot)
                for copy in gu_copies(j, slot):
                    copy.wait()
                for m in range(2):
                    got = (jnp.dot(rows_of(0), wgb[slot, m, :quarter, :], preferred_element_type=F32)
                           + jnp.dot(rows_of(1), wgb[slot, m, quarter:, :], preferred_element_type=F32))
                    for i, u in enumerate(units_of):
                        if part == 0:
                            ps[u, j, m] = got[i * half_rows:(i + 1) * half_rows].astype(BF)
                        else:
                            own[u, j - n_half, m] = got[i * half_rows:(i + 1) * half_rows]
                if part == 0:
                    p_copy(units_of[0], j).start()
                return 0
            lax.fori_loop(part * n_half, (part + 1) * n_half, step, 0)
            if part == 0:
                for u in units_of[1:]:
                    for j in range(n_half):
                        p_copy(u, j).start()

        def arrived(half):
            at = pl.ds(pl.multiple_of(half * half_rows, half_rows), half_rows)
            return lambda q: xg[0, q, at, :]

        def h_copy(u, j, half):
            piece = hid.at[u, half * n_half + j]
            return remote(piece, piece, h_s.at[u, j], h_r.at[u, j], dp=ox)

        def hidden(u):
            def step(j, _):
                p_copy(u, j).wait_recv()
                gate = own[u, j, 0] + pr[u, j, 0].astype(F32)
                up = own[u, j, 1] + pr[u, j, 1].astype(F32)
                hid[u, x * n_half + j] = (gate / (1.0 + jnp.exp(-gate)) * up).astype(BF)
                h_copy(u, j, x).start()
                return 0
            lax.fori_loop(0, n_half, step, 0)

        def hidden_arrival(u):
            def step(j, _):
                h_copy(u, j, ox).wait_recv()
                return 0
            lax.fori_loop(0, n_half, step, 0)

        def chooser(b):
            at = jnp.where(x == b, order[...], order2[...])[0:1, :]
            match = (lax.broadcasted_iota(jnp.int32, (rows, rows), 0) == at).astype(F32)
            return jnp.transpose(match).astype(BF)

        def sort_hidden():
            chosen = chooser(0)
            for k in range(2 * n_half):
                sh[:, k * wide:(k + 1) * wide] = (
                    jnp.dot(chosen[:, :half_rows], hid[0, k], preferred_element_type=F32)
                    + jnp.dot(chosen[:, half_rows:], hid[1, k], preferred_element_type=F32)).astype(BF)

        def sort_tokens():
            chosen = chooser(1)
            for q in range(2):
                for k in range(0, quarter, span):
                    moved = jnp.dot(chosen, xg[1, q, :, k:k + span], preferred_element_type=F32).astype(BF)
                    xt[q, :, k:k + span] = moved

        def in_order(u):
            for k in range(2 * n_half):
                sh[:half_rows, k * wide:(k + 1) * wide] = hid[u, k]

        def q_copy(u, n):
            return remote(qs.at[u, n], qr.at[u, n], q_s.at[u, n], q_r.at[u, n], pair=oc)

        low, high = lax.rem(z, 2), z // 2

        def near_copy(u, n):
            mine = zs.at[u, n, pl.ds(pl.multiple_of((1 - low) * 2 * share, 2 * share), 2 * share)]
            return remote(mine, zr.at[u, n], n_s.at[u, n], n_r.at[u, n], tensor=z + 1 - 2 * low)

        def far_copy(u, n):
            mine = zs2.at[u, n, pl.ds(pl.multiple_of((1 - high) * share, share), share)]
            return remote(mine, zr2.at[u, n], z_s.at[u, n], z_r.at[u, n], tensor=lax.rem(z + 2, n_z))

        def reduce(units_of, n):
            slot = lax.rem(n, 2)
            for i, u in enumerate(units_of):
                q_copy(u, n).wait_recv()
                total = keep[slot, i] + qr[u, n].astype(F32)
                zs[u, n] = total.astype(BF)
                near_copy(u, n).start()
                keep[slot, i] = total
                acc[u, n] = keep[slot, i, pl.ds(pl.multiple_of(low * 2 * share, 2 * share), 2 * share), :]

        def relay(u, n):
            near_copy(u, n).wait_recv()
            total = acc[u, n] + zr[u, n].astype(F32)
            acc[u, n] = total
            zs2[u, n] = total.astype(BF)
            far_copy(u, n).start()

        def relays(u):
            def step(n, _):
                relay(u, n)
                return 0
            lax.fori_loop(0, n_out, step, 0)

        def down(units_of, loads=False, passing=None):
            many = len(units_of)

            def step(n, _):
                slot = lax.rem(n, 2)
                if loads:
                    down_copy(n).wait()
                part = jnp.dot(sh[:many * half_rows, :], wdb[n], preferred_element_type=F32)
                for i, u in enumerate(units_of):
                    qs[u, n] = part[i * half_rows + kept:(i + 1) * half_rows].astype(BF)
                    q_copy(u, n).start()
                    keep[slot, i] = part[i * half_rows:i * half_rows + kept]
                pl.when(n >= 1)(lambda: reduce(units_of, n - 1))
                if passing is not None:
                    relay(passing, n)
                return 0
            lax.fori_loop(0, n_out, step, 0)
            reduce(units_of, n_out - 1)

        def f_copy(h, n):
            return remote(fs.at[h, n], fr.at[h, n], f_s.at[h, n], f_r.at[h, n], dp=ox)

        def finish(u):
            b, h = u // 2, u % 2

            def step(n, _):
                far_copy(u, n).wait_recv()
                total = acc[u, n, pl.ds(pl.multiple_of(high * share, share), share), :] + zr2[u, n].astype(F32)

                @pl.when(x == b)
                def _():
                    out[h * share:(h + 1) * share,
                        pl.ds(pl.multiple_of(b * out_w + n * span, span), span)] = total.astype(BF)

                @pl.when(x != b)
                def _():
                    fs[h, n] = total.astype(BF)
                    f_copy(h, n).start()
                return 0
            lax.fori_loop(0, n_out, step, 0)

        side = z // near
        own_sends(0)
        for d in range(1, near):
            hop(0, d)
        siblings(0, side)
        gate_up((side,), arrived(side), 0)
        hop(0, near)
        gate_up((side,), arrived(side), 1)
        for d in range(near + 1, n_z):
            hop(0, d)
        own_sends(1)
        siblings(0, 1 - side)
        gate_up((1 - side,), arrived(1 - side), 0)
        for d in range(1, near):
            hop(1, d)
        hidden(side)
        gate_up((1 - side,), arrived(1 - side), 1)
        down_load()
        hop(1, near)
        for d in range(near + 1, n_z):
            hop(1, d)
        siblings(1, 0)
        siblings(1, 1)
        o_copy.wait_recv()
        sort_tokens()
        hidden(1 - side)
        gate_up((2, 3), lambda q: xt[q], 0)
        hidden_arrival(0)
        hidden_arrival(1)
        sort_hidden()
        down((0, 1), True)
        gate_up((2, 3), lambda q: xt[q], 1, True)
        hidden(2)
        hidden(3)
        relays(0)
        relays(1)
        hidden_arrival(2)
        in_order(2)
        down((2,))
        hidden_arrival(3)
        in_order(3)
        down((3,), passing=2)
        finish(0)
        finish(1)
        relays(3)
        finish(2)
        finish(3)

        for h in range(2):
            def last(n, _):
                f_copy(h, n).wait_recv()
                out[h * share:(h + 1) * share,
                    pl.ds(pl.multiple_of(ox * out_w + n * span, span), span)] = fr[h, n]
                return 0
            lax.fori_loop(0, n_out, last, 0)

        x_copy.wait_send()
        o_copy.wait_send()
        for b in range(2):
            for d in range(n_z):
                ag_each(b, d, sent)

        def sent_unit(u, _):
            def sent_x(j, _):
                p_copy(u, j).wait_send()
                h_copy(u, j, x).wait_send()
                return 0
            lax.fori_loop(0, n_half, sent_x, 0)

            def sent_z(n, _):
                q_copy(u, n).wait_send()
                near_copy(u, n).wait_send()
                far_copy(u, n).wait_send()
                return 0
            lax.fori_loop(0, n_out, sent_z, 0)
            return 0
        lax.fori_loop(0, 4, sent_unit, 0)

        def sent_f(n, _):
            f_copy(0, n).wait_send()
            f_copy(1, n).wait_send()
            return 0
        lax.fori_loop(0, n_out, sent_f, 0)

    z, c = lax.axis_index("tensor"), lax.axis_index("pair")
    kinds = lax.dynamic_slice_in_dim(modality, z * held, held, 0)
    kinds = jnp.broadcast_to(kinds[:, None], (held, 128))
    order = time_order.reshape(2, 2, 2, 2, share).transpose(3, 2, 1, 0, 4)
    order = jnp.where(c == 0, order, order[:, ::-1]).reshape(1, rows)
    order = jnp.broadcast_to(order, (8, rows))
    vmem, anywhere = pl.BlockSpec(memory_space=pltpu.VMEM), pl.BlockSpec(memory_space=pl.ANY)
    dma = pltpu.SemaphoreType.DMA
    scratch = [
        pltpu.VMEM((held, quarter), BF),
        pltpu.VMEM((2, 2, rows, quarter), BF),
        pltpu.VMEM((2, rows, quarter), BF),
        pltpu.VMEM((8, rows), jnp.int32),
        pltpu.VMEM((2, 2, depth, wide), BF),
        pltpu.VMEM((n_out, units, span), BF),
        pltpu.VMEM((4, n_half, 2, half_rows, wide), BF),
        pltpu.VMEM((4, n_half, 2, half_rows, wide), BF),
        pltpu.VMEM((4, n_half, 2, half_rows, wide), F32),
        pltpu.VMEM((4, 2 * n_half, half_rows, wide), BF),
        pltpu.VMEM((rows, units), BF),
        pltpu.VMEM((4, n_out, kept, span), BF),
        pltpu.VMEM((4, n_out, kept, span), BF),
        pltpu.VMEM((2, 2, kept, span), F32),
        pltpu.VMEM((4, n_out, kept, span), BF),
        pltpu.VMEM((4, n_out, 2 * share, span), BF),
        pltpu.VMEM((4, n_out, 2 * share, span), BF),
        pltpu.VMEM((4, n_out, share, span), BF),
        pltpu.VMEM((4, n_out, 2 * share, span), F32),
        pltpu.VMEM((2, n_out, share, span), BF),
        pltpu.VMEM((2, n_out, share, span), BF),
        dma((2, 2)), dma((n_out,)), dma, dma, dma, dma,
        dma((2, n_z, 3)), dma((2, n_z)), dma((2, n_z)),
        dma((4, n_half)), dma((4, n_half)), dma((4, n_half)), dma((4, n_half)),
        dma((4, n_out)), dma((4, n_out)), dma((4, n_out)), dma((4, n_out)), dma((4, n_out)), dma((4, n_out)),
        dma((2, n_out)), dma((2, n_out)),
    ]
    return pl.pallas_call(
        kernel,
        out_shape=jax.ShapeDtypeStruct((rows // (n_z * 2), width), BF),
        in_specs=[vmem, vmem, vmem, vmem, anywhere, anywhere, anywhere],
        out_specs=vmem,
        scratch_shapes=scratch,
        compiler_params=pltpu.CompilerParams(
            collective_id=0, has_side_effects=True, vmem_limit_bytes=60 * 2**20),
        cost_estimate=pl.CostEstimate(
            flops=12 * rows * depth * units, bytes_accessed=12 * depth * units, transcendentals=0),
    )(tokens, kinds, order, norm_gain, gate_weight, up_weight, down_weight)


def solution(mesh):
    placed = (
        P(("groups", "dp", "tensor"), None),
        P(("groups", "dp")),
        P(("groups", "dp")),
        P(),
        P("dp", ("tensor", "pair")),
        P("dp", ("tensor", "pair")),
        P(("tensor", "pair"), "dp"),
    )

    def per_device(*arrays):
        share = arrays[1].shape[0] // (mesh.shape["tensor"] * mesh.shape["pair"])
        if mesh.shape["dp"] == 2 and mesh.shape["pair"] == 2 and mesh.shape["tensor"] == 4 and share % 32 == 0:
            return fused(mesh, *arrays)
        return plain(mesh, *arrays)

    return jax.shard_map(
        per_device,
        mesh=mesh,
        in_specs=placed,
        out_specs=P(("groups", "dp", "tensor", "pair"), None),
        check_vma=False,
    )
```
